1024 devices in a mesh: lat: 64 (over z, core), lon: 16 (over x, y).
Axes of the slice: x: 4, y: 4, z: 32, core: 2. Of those that a mesh axis runs over, the one named last changes fastest.
Arguments:
- spectral: bfloat16 [640, 2, 128, 640], P('lat', None, 'lon'), may hold values from -6 to 6
- wavenumber_of_slot: int32 [640], replicated, may hold values from 0 to 639, each once
- filter_strength: float32 [128], P('lon'), may hold values from 0.1 to 10
- courant: bfloat16 [2, 640, 1280, 128], P(None, 'lat', 'lon'), may hold values from -0.59765625 to 0.59765625
- sunlit_blocks: int32 [64, 16, 12], P('lat', 'lon'), may hold values from 0 to 49, as said below
- sunlit_owner: int32 [64, 16, 12, 1], P('lat', 'lon'), may hold values from 0 to 15; in each aligned block of 12 rows (0 to 11, 12 to 23, ..., all dimensions but the last counted through in order) at most 2 rows name the same one
- radiation_in: bfloat16 [16, 128, 512], P('lon'), may hold values from -0.5 to 0.5
- radiation_mid: bfloat16 [16, 512, 512], P('lon'), may hold values from -0.25 to 0.25
- radiation_out: bfloat16 [16, 512, 128], P('lon'), may hold values from -0.25 to 0.25
Outputs:
- advected: float32 [640, 1280, 128], P('lat', 'lon')
- heating: bfloat16 [640, 1280, 128], P('lat', 'lon')
The draws below stay inside these ranges and needn't reach their ends.
Inputs may be any that keep to these rules, and one draw needn't show every extreme that they name: `wavenumber_of_slot`: each of 0 to 639 exactly once. `sunlit_blocks`: the 12 block numbers of one device are distinct. `sunlit_owner`: among the 12 blocks of one device no regime appears more than 2 times, and some device names some regime exactly 2 times.
All inputs are finite; a program needn't handle non-finite values.
Results may differ from the reference program's by a relative error of at most 0.015.
Values may be sent and summed in bfloat16 or wider, within the bound.
A program may use at most 32 MiB of HBM per device.

```python
import math
import jax
import jax.numpy as jnp
import numpy as np
from jax import lax

TRUNC = 640
NLAT = 640
NLON = 1280
LEV = 128
HID = 512
BC = 16
CAP = 2
SUNLIT = 12
LATD = 10
LOND = 80
NB = 5
BLK_DEV = 50
REGIMES = 16
N_LAT = 64
N_LON = 16


def pick_blocks(device_key):
    return jax.random.permutation(device_key, BLK_DEV)[:SUNLIT]


def draw_sunlit_blocks(key, part):
    device_keys = jax.random.split(jax.random.fold_in(key, 7), N_LAT * N_LON)
    picks = jax.vmap(pick_blocks)(device_keys)
    return picks.astype(jnp.int32).reshape(N_LAT, N_LON, SUNLIT)


def block_levels(stream_key, shape, pieces, low, high):
    def one(dim, blocks):
        draws = jax.random.uniform(jax.random.fold_in(jax.random.fold_in(stream_key, 6), dim), (blocks,), jnp.float32, low / len(pieces), high / len(pieces))
        return jnp.repeat(jnp.exp(draws), shape[dim] // blocks).reshape((-1,) + (1,) * (len(shape) - dim - 1))

    loudness = one(*pieces[0])
    for cut in pieces[1:]:
        loudness = loudness * one(*cut)
    return loudness


def deal_out(rng, own, number, rows, number_of, top, most, skew):
    ranking = jax.random.permutation(rng, number_of)
    packed, common = shares(number_of, rows * top, most, skew, True), shares(number_of, rows * top, most, skew, False)
    places = jnp.arange(number_of)

    def named(lengths, rotation):
        used = int((lengths > 0).sum())
        fixed = max(1, used // 4)
        passed = fixed + (places - fixed + rotation * (used - fixed)) % max(1, number_of - fixed)
        return jnp.zeros((number_of,), jnp.int32).at[ranking[jnp.where(places < fixed, places, passed)]].set(jnp.asarray(lengths, jnp.int32))

    lengths = jnp.where(number % 4 == 0, named(packed, number // 4), named(common, number - number // 4 - 1))
    mixed = jax.random.permutation(jax.random.fold_in(own, 3), number_of)
    donor, sink = mixed[0:number_of // 2 * 2:2], mixed[1:number_of // 2 * 2:2]
    room = jnp.minimum(lengths[donor] - 1, most - lengths[sink]) // 2
    room = jnp.where((donor == ranking[0]) | (sink == ranking[0]) | (lengths[sink] == 0), 0, jnp.maximum(room, 0))
    passed = jax.random.randint(jax.random.fold_in(own, 4), (number_of // 2,), 0, 1 << 20) % (room + 1)
    lengths = lengths.at[donor].add(-passed).at[sink].add(passed)
    items = jnp.searchsorted(jnp.cumsum(lengths), jnp.arange(rows * top), side="right").astype(jnp.int32)
    table = items.reshape(top, rows).T
    table = table[jax.random.permutation(jax.random.fold_in(own, 1), rows)]
    rotation = jax.random.randint(jax.random.fold_in(own, 2), (rows, 1), 0, top)
    return jnp.take_along_axis(table, (jnp.arange(top)[None, :] + rotation) % top, axis=1)


def shares(amount, total, bound, slope, full):
    loads = [(1 << 20) // math.isqrt(grade ** slope) + 1 for grade in range(1, amount + 1)]
    largest = bound if full else min(bound, max(-(-total // amount), total * loads[0] // sum(loads)))
    least = 1 if total - largest >= amount - 1 else 0
    counts, spare = [largest] + [least] * (amount - 1), total - largest - least * (amount - 1)
    while spare > 0:
        candidates = [i for i in range(1, amount) if counts[i] < largest] or [i for i in range(1, amount) if counts[i] < bound]
        whole, left = sum([loads[i] for i in candidates]), spare
        for i in candidates:
            more = min(bound - counts[i], max(1, left * loads[i] // whole), spare)
            counts[i] = counts[i] + more
            spare = spare - more
    return np.array(counts)


def bell_draw(stream_key, shape, spread, most, pieces=(), held_as=jnp.bfloat16):
    drawn = spread * jax.random.normal(stream_key, shape, jnp.float32)
    if pieces:
        drawn = drawn * block_levels(stream_key, shape, pieces, -0.22, 0.18)
    return jnp.clip(drawn, -most, most).astype(held_as)


def setup_inputs(seed: int = 0) -> dict:
    key_of = jax.random.split(jax.random.key(seed), 10)
    spectral = bell_draw(key_of[0], (TRUNC, 2, LEV, TRUNC), 1.0, 6.0, ((0, 64), (2, 16)))
    wavenumber_of_slot = jax.random.permutation(key_of[1], TRUNC).astype(jnp.int32)
    filter_strength = jnp.clip(jnp.exp(math.log(10.0) - 4.6051702 * jax.random.uniform(key_of[2], (LEV,), jnp.float32) ** block_levels(key_of[2], (LEV,), ((0, 16),), -0.2, 0.2)), 0.1, 10.0)
    courant = jnp.clip(jax.random.uniform(key_of[3], (2, NLAT, NLON, LEV), jnp.float32, -0.59765625, 0.59765625) * block_levels(key_of[3], (2, NLAT, NLON, LEV), ((1, 64), (2, 16)), -0.4, 0.0), -0.59765625, 0.59765625).astype(jnp.bfloat16)
    sunlit_blocks = draw_sunlit_blocks(jax.random.fold_in(key_of[9], 71), 0)
    sunlit_owner_keys = jax.random.split(jax.random.fold_in(key_of[5], 1), N_LAT * N_LON * SUNLIT // SUNLIT)
    sunlit_owner_turns = jax.random.permutation(jax.random.fold_in(key_of[5], 3), N_LAT * N_LON * SUNLIT // SUNLIT)
    sunlit_owner = jax.vmap(lambda own, number: deal_out(jax.random.fold_in(key_of[5], 2), own, number, SUNLIT, REGIMES, 1, CAP, 2))(sunlit_owner_keys, sunlit_owner_turns).reshape((N_LAT, N_LON, SUNLIT, 1))
    radiation_in = bell_draw(key_of[6], (REGIMES, LEV, HID), LEV ** -0.5, 0.5, ((0, 16),))
    radiation_mid = bell_draw(key_of[7], (REGIMES, HID, HID), HID ** -0.5, 0.25, ((0, 16),))
    radiation_out = bell_draw(key_of[8], (REGIMES, HID, LEV), HID ** -0.5, 0.25, ((0, 16),))
    return dict(spectral=spectral, wavenumber_of_slot=wavenumber_of_slot, filter_strength=filter_strength, courant=courant, sunlit_blocks=sunlit_blocks, sunlit_owner=sunlit_owner, radiation_in=radiation_in, radiation_mid=radiation_mid, radiation_out=radiation_out)


group_rows = 64

def latitude_table(degrees, latitudes):
    degree_grid = lax.broadcasted_iota(jnp.int32, (degrees, latitudes), 0)
    row_index = lax.broadcasted_iota(jnp.int32, (degrees, latitudes), 1)
    phase_count = degree_grid * (2 * row_index + 1) % (4 * latitudes)
    phase_angle = phase_count.astype(jnp.float32) * (math.pi / (2.0 * latitudes))
    return (jnp.cos(phase_angle) * math.sqrt(2.0 / degrees)).astype(jnp.bfloat16)

def longitude_table(zonal_waves, longitudes):
    total_count = zonal_waves.shape[0]
    column_index = lax.broadcasted_iota(jnp.int32, (total_count, longitudes), 1)
    phase_count = zonal_waves.astype(jnp.int32)[:, None] * column_index % longitudes
    phase_angle = phase_count.astype(jnp.float32) * (2.0 * math.pi / longitudes)
    scaling = 1.0 / math.sqrt(total_count)
    return jnp.stack([jnp.cos(phase_angle) * scaling, -jnp.sin(phase_angle) * scaling], axis=1).astype(jnp.bfloat16)

def damped(spectral, zonal_waves, strength, degrees):
    degree_grid = lax.broadcasted_iota(jnp.int32, spectral.shape, 3)
    component = lax.broadcasted_iota(jnp.int32, spectral.shape, 1)
    zonal_order = zonal_waves.astype(jnp.int32)[:, None, None, None]
    retained = (degree_grid >= zonal_order) & ((component == 0) | (zonal_order > 0))
    relative = (degree_grid * (degree_grid + 1)).astype(jnp.float32) / float(degrees * (degrees + 1))
    factor = 1.0 / (1.0 + strength[None, None, :, None] * relative * relative)
    return jnp.where(retained, spectral.astype(jnp.float32) * factor, 0.0).astype(jnp.bfloat16)

def transport(padded, zonal, meridional):
    centre = padded[1:-1, 1:-1]
    northern = padded[2:, 1:-1]
    southern = padded[:-2, 1:-1]
    eastern = padded[1:-1, 2:]
    western = padded[1:-1, :-2]
    along = centre - 0.5 * zonal * (eastern - western) + 0.5 * zonal * zonal * (eastern - 2.0 * centre + western)
    return along - 0.5 * meridional * (northern - southern) + 0.5 * meridional * meridional * (northern - 2.0 * centre + southern)

def advect(tracer, zonal, meridional):
    padded = jnp.pad(tracer, ((1, 1), (0, 0), (0, 0)))
    padded = jnp.concatenate([padded[:, -1:], padded, padded[:, :1]], axis=1)
    return transport(padded, zonal, meridional)

def regime_net(columns, w_in, w_mid, w_out):
    layer_one = jax.nn.silu(jnp.dot(columns, w_in, preferred_element_type=jnp.float32)).astype(jnp.bfloat16)
    layer_two = jax.nn.silu(jnp.dot(layer_one, w_mid, preferred_element_type=jnp.float32)).astype(jnp.bfloat16)
    return jnp.dot(layer_two, w_out, preferred_element_type=jnp.float32).astype(jnp.bfloat16)

def reference(spectral, wavenumber_of_slot, filter_strength, courant, sunlit_blocks, sunlit_owner, radiation_in, radiation_mid, radiation_out):
    filtered = damped(spectral, wavenumber_of_slot, filter_strength, TRUNC)
    coefficients = jnp.dot(filtered.reshape(-1, TRUNC), latitude_table(TRUNC, NLAT), preferred_element_type=jnp.float32)
    coefficients = coefficients.astype(jnp.bfloat16).reshape(TRUNC, 2, LEV, NLAT)
    wave_table = longitude_table(wavenumber_of_slot, NLON)
    grid_field = jnp.einsum('sclj,sck->jkl', coefficients.astype(jnp.float32), wave_table.astype(jnp.float32), precision=lax.Precision.HIGHEST).astype(jnp.bfloat16)
    zonal = courant[0].astype(jnp.float32)
    meridional = courant[1].astype(jnp.float32)
    advected = advect(advect(grid_field.astype(jnp.float32), zonal, meridional), zonal, meridional)
    state = advected.astype(jnp.bfloat16)
    sunlit = sunlit_blocks.reshape(-1).astype(jnp.int32)
    destination = sunlit_owner.reshape(-1).astype(jnp.int32)
    total_rows = sunlit.shape[0]
    device = jnp.arange(total_rows, dtype=jnp.int32) // SUNLIT
    latitude_row = device // N_LON * LATD + sunlit // NB
    first_lon = device % N_LON * LOND + sunlit % NB * BC
    lon_index = first_lon[:, None] + jnp.arange(BC, dtype=jnp.int32)[None, :]
    picked = state[latitude_row[:, None], lon_index]
    order = jnp.argsort(destination, stable=True).astype(jnp.int32)
    ranked = picked[order]
    group_sizes = lax.optimization_barrier(jnp.sum((destination[:, None] == jnp.arange(REGIMES, dtype=jnp.int32)[None, :]).astype(jnp.int32), axis=0))
    starts = (jnp.cumsum(group_sizes) - group_sizes).astype(jnp.int32)

    def regime_body(regime, result):
        w_in = radiation_in[regime]
        w_mid = radiation_mid[regime]
        w_out = radiation_out[regime]

        def block_body(sweep, total):
            offsets = jnp.arange(group_rows, dtype=jnp.int32)
            usable = sweep * group_rows + offsets < group_sizes[regime]
            take_index = jnp.minimum(starts[regime] + sweep * group_rows + offsets, total_rows - 1).astype(jnp.int32)
            columns = ranked[take_index].reshape(group_rows * BC, LEV)
            output = regime_net(columns, w_in, w_mid, w_out).astype(jnp.float32).reshape(group_rows, BC * LEV)
            output = jnp.where(usable[:, None], output, 0.0)
            return total.at[order[take_index]].add(output)
        block_total = ((group_sizes[regime] + group_rows - 1) // group_rows).astype(jnp.int32)
        return lax.fori_loop(jnp.int32(0), block_total, block_body, result)
    result = lax.fori_loop(0, REGIMES, regime_body, jnp.zeros((total_rows, BC * LEV), jnp.float32))
    heating = jnp.zeros((NLAT, NLON, LEV), jnp.float32).at[latitude_row[:, None], lon_index].set(result.reshape(total_rows, BC, LEV))
    return (advected, heating.astype(jnp.bfloat16))
```

```python
import functools
import math

import jax
import jax.numpy as jnp
import numpy as np
from jax import lax
from jax.experimental import pallas as pl
from jax.experimental.pallas import tpu as pltpu
from jax.sharding import PartitionSpec as P

MESH = pl.DeviceIdType.MESH
F32 = jnp.float32
BF16 = jnp.bfloat16

DEG = 640
NLON = 1280
LAT = 64
LON = 16
ROWS = 10
COLS = 80
LEV = 128
OWN = 8
LEAD = 8
WIDE = 96
HID = 512


def latitude_rows():
    row = np.arange(LAT * 16) % 16
    j = np.arange(LAT * 16) // 16 * ROWS + np.where(row < ROWS, row, row - ROWS)
    n = np.arange(DEG)
    phase = (n[None, :] * (2 * j[:, None] + 1)) % (4 * DEG)
    table = np.cos(phase * (math.pi / (2.0 * DEG))) * math.sqrt(2.0 / DEG)
    return table.astype(np.float32).astype(jnp.bfloat16)


def circle(turns):
    y = turns * math.pi
    z = y * y
    s = 1.0
    for k in (11, 9, 7, 5, 3):
        s = 1.0 - z * s * (1.0 / (k * (k - 1)))
    s = s * y
    c = 1.0
    for k in (12, 10, 8, 6, 4, 2):
        c = 1.0 - z * c * (1.0 / (k * (k - 1)))
    return 1.0 - 2.0 * s * s, 2.0 * s * c


def fraction(product):
    turns = product * (1.0 / NLON)
    return turns - jnp.floor(turns + 0.5)


def silu(v):
    return v / (1.0 + jnp.exp(-v))


def peer_at(t, p):
    i = t // 2
    far = 16 - (i + 1) // 2
    chip = lax.rem(p // 2 + jnp.where(i % 2 == 1, far, 32 - far), 32)
    core = jnp.where(t == 62, 1 - lax.rem(p, 2), lax.rem(t, 2))
    return jnp.where(t == 62, p // 2, chip) * 2 + core


def kernel(
    wave_ref,
    strength_ref,
    sunlit_ref,
    owner_ref,
    spectral_hbm,
    table_hbm,
    courant_hbm,
    win_hbm,
    wmid_hbm,
    wout_hbm,
    advected_hbm,
    heating_hbm,
    spec,
    table,
    cour,
    w_in,
    w_mid,
    w_out,
    damp,
    pay,
    got,
    gotf,
    wide,
    trig,
    mcol,
    slab,
    land,
    c_north,
    c_south,
    c_west,
    c_east,
    flow,
    q_zero,
    q_one,
    adv,
    state,
    out_slots,
    in_slots,
    back_slots,
    ret_slots,
    heat,
    pick,
    place,
    local_sem,
    send_sem,
    recv_sem,
):
    p = lax.axis_index("lat")
    q = lax.axis_index("lon")
    north = lax.rem(p + 1, LAT)
    south = lax.rem(p + LAT - 1, LAT)
    east = lax.rem(q + 1, LON)
    west = lax.rem(q + LON - 1, LON)

    get_spec = pltpu.make_async_copy(spectral_hbm, spec, local_sem.at[0])
    get_table = pltpu.make_async_copy(table_hbm, table, local_sem.at[1])
    get_cour = pltpu.make_async_copy(courant_hbm, cour, local_sem.at[2])
    get_in = pltpu.make_async_copy(win_hbm, w_in, local_sem.at[3])
    get_mid = pltpu.make_async_copy(wmid_hbm, w_mid, local_sem.at[4])
    get_out = pltpu.make_async_copy(wout_hbm, w_out, local_sem.at[5])
    get_spec.start()
    get_table.start()

    barrier = pltpu.get_barrier_semaphore()

    def greet_lat(t, carry):
        pl.semaphore_signal(barrier, inc=1, device_id=(peer_at(t, p), q), device_id_type=MESH)
        return carry

    lax.fori_loop(0, LAT - 1, greet_lat, 0)

    def greet_lon(t, carry):
        other = lax.rem(q + t, LON)
        for row in (p, north, south):
            pl.semaphore_signal(barrier, inc=1, device_id=(row, other), device_id_type=MESH)
        return carry

    lax.fori_loop(1, LON, greet_lon, 0)

    get_cour.start()
    get_in.start()
    get_mid.start()
    get_out.start()

    degree = lax.broadcasted_iota(jnp.int32, (OWN, DEG), 1)
    level = lax.broadcasted_iota(jnp.int32, (OWN, DEG), 0)
    strength = jnp.zeros((OWN, DEG), F32)
    for l in range(OWN):
        strength = jnp.where(level == l, strength_ref[l], strength)
    relative = (degree * (degree + 1)).astype(F32) / float(DEG * (DEG + 1))
    factor = 1.0 / (1.0 + strength * relative * relative)
    get_spec.wait()
    for s in range(ROWS):
        wave = wave_ref[p * ROWS + s]
        real = jnp.where(degree >= wave, spec[s, 0].astype(F32) * factor, 0.0)
        imag = jnp.where(
            degree >= jnp.where(wave > 0, wave, DEG), spec[s, 1].astype(F32) * factor, 0.0
        )
        both = jnp.concatenate([real, imag], axis=0).astype(BF16)
        damp[pl.ds(s * 16, 16), :] = both
        if s >= 8:
            damp[pl.ds(s * 16 + 32, 16), :] = both
    damp[pl.ds(192, 64), :] = jnp.zeros((64, DEG), BF16)

    get_table.wait()
    row16 = lax.broadcasted_iota(jnp.int32, (128, LEV), 0) % 16
    lane = lax.broadcasted_iota(jnp.int32, (128, LEV), 1)

    def over_degrees(t, carry):
        rows = table[pl.ds(pl.multiple_of(t * 128, 128), 128), :]
        y = lax.dot_general(rows, damp[...], (((1,), (1,)), ((), ())), preferred_element_type=F32)
        first, last = y[:, :128], y[:, 128:]
        tail = jnp.where(lane < 32, last, pltpu.roll(last, 6, 0))
        packed = jnp.where(row16 < ROWS, first, tail).astype(BF16)
        pay[pl.ds(t * 8, 8)] = packed.reshape(8, 16, LEV)
        return carry

    lax.fori_loop(0, 8, over_degrees, 0)

    sub8 = lax.broadcasted_iota(jnp.int32, (8, LEV), 0)

    def columns(t, carry):
        s, group = t // 8, lax.rem(t, 8)
        value = jnp.zeros((8, LEV), jnp.int32)
        for r in range(8):
            value = jnp.where(sub8 == r, wave_ref[(group * 8 + r) * ROWS + s], value)
        mcol[pl.ds(pl.multiple_of(t * 8, 8), 8), :] = value.astype(F32)
        return carry

    lax.fori_loop(0, 80, columns, 0)

    shift = (lax.broadcasted_iota(jnp.int32, (64, LEV), 1) - LEAD).astype(F32)
    scale = 1.0 / math.sqrt(DEG)

    def trig_rows(s, carry):
        m = mcol[pl.ds(pl.multiple_of(s * 64, 64), 64), :]
        c, d = circle(fraction(m * shift))
        c, d = c * scale, d * scale
        c1, d1 = circle(fraction(m * float(COLS)))
        base = pl.multiple_of(s * 128, 128)
        for other in range(LON):
            lanes = pl.ds((other % 2) * 128, 128)
            trig[other // 2, pl.ds(base, 64), lanes] = c.astype(BF16)
            trig[other // 2, pl.ds(base + 64, 64), lanes] = (-d).astype(BF16)
            c, d = c * c1 - d * d1, d * c1 + c * d1
        return carry

    lax.fori_loop(0, ROWS, trig_rows, 0)

    def clear_pick(t, carry):
        pick[t] = 0
        return carry

    owners = [owner_ref[t] for t in range(12)]
    listed = [sunlit_ref[t] for t in range(12)]
    slots = []
    for t in range(12):
        rank = jnp.int32(0)
        for u in range(t):
            rank = rank + (owners[u] == owners[t]).astype(jnp.int32)
        slots.append(owners[t] * 2 + rank)

    def fill_pick(k, carry):
        value = jnp.int32(0)
        for t in range(12):
            value = jnp.where(slots[t] == k, listed[t], value)
        pick[k] = value
        return carry

    lax.fori_loop(0, 32, fill_pick, 0)

    def fill_place(k, carry):
        value = jnp.int32(32)
        for t in range(12):
            value = jnp.where(listed[t] == k, slots[t], value)
        place[k] = value
        return carry

    lax.fori_loop(0, 50, fill_place, 0)

    get_cour.wait()
    pl.semaphore_wait(barrier, LAT - 1 + 3 * (LON - 1))

    def send_lat(t, carry):
        other = peer_at(t, p)
        pltpu.make_async_remote_copy(
            pay.at[other],
            got.at[p],
            send_sem.at[0],
            recv_sem.at[0],
            device_id=(other, q),
            device_id_type=MESH,
        ).start()
        return carry

    lax.fori_loop(0, LAT - 1, send_lat, 0)
    pltpu.make_async_copy(pay.at[p], got.at[p], recv_sem.at[0]).start()

    edges = [
        pltpu.make_async_remote_copy(
            cour.at[:, ROWS - 1],
            c_south,
            send_sem.at[1],
            recv_sem.at[1],
            device_id=(north, q),
            device_id_type=MESH,
        ),
        pltpu.make_async_remote_copy(
            cour.at[:, 0],
            c_north,
            send_sem.at[2],
            recv_sem.at[2],
            device_id=(south, q),
            device_id_type=MESH,
        ),
        pltpu.make_async_remote_copy(
            cour.at[:, :, pl.ds(COLS - 16, 16), :],
            c_west,
            send_sem.at[3],
            recv_sem.at[3],
            device_id=(p, east),
            device_id_type=MESH,
        ),
        pltpu.make_async_remote_copy(
            cour.at[:, :, pl.ds(0, 16), :],
            c_east,
            send_sem.at[4],
            recv_sem.at[4],
            device_id=(p, west),
            device_id_type=MESH,
        ),
    ]
    for edge in edges:
        edge.start()
    for edge in edges:
        edge.wait()
    zeros8 = jnp.zeros((8, LEV), F32)
    for k in range(2):
        flow[k, 0] = jnp.concatenate([zeros8, c_south[k].astype(F32), zeros8], axis=0)
        flow[k, ROWS + 1] = jnp.concatenate([zeros8, c_north[k].astype(F32), zeros8], axis=0)

    def fill_flow(r, carry):
        for k in range(2):
            flow[k, r + 1] = jnp.concatenate(
                [
                    c_west[k, r].astype(F32)[8:],
                    cour[k, r].astype(F32),
                    c_east[k, r].astype(F32)[:8],
                ],
                axis=0,
            )
        return carry

    lax.fori_loop(0, ROWS, fill_flow, 0)

    pltpu.make_async_copy(got, got, recv_sem.at[0]).wait()
    gotf[...] = got[...].astype(F32).reshape(LAT * 16, LEV)
    low = lax.broadcasted_iota(jnp.int32, (8, LEV), 1) < 64
    for r in range(16):
        part = gotf[pl.ds(r, LAT, stride=16), :]
        turned = jnp.concatenate([part, part], axis=0).T
        if r < ROWS:
            for a in range(8):
                wide[pl.ds(r * 8, 8), pl.ds(a * 128, 128)] = jnp.where(
                    low, turned[a * 16 : a * 16 + 8], turned[a * 16 + 8 : a * 16 + 16]
                )
        else:
            for g, jj in ((0, r - ROWS), (1, r - ROWS + 4)):
                if g == 1 and jj < 6:
                    continue
                for a in range(2):
                    at = g * 32 + a * 16
                    wide[pl.ds(jj * 8, 8), pl.ds((8 + a) * 128, 128)] = jnp.where(
                        low, turned[at : at + 8], turned[at + 8 : at + 16]
                    )

    def send_lon(t, carry):
        pair = lax.rem(q // 2 + t, LON // 2)
        g = jnp.dot(wide[...].astype(BF16), trig[pair], preferred_element_type=F32).astype(BF16)
        for h in range(2):
            other = pair * 2 + h
            slab[other] = g[:, h * 128 : (h + 1) * 128]

            @pl.when(other != q)
            def _():
                pltpu.make_async_remote_copy(
                    slab.at[other],
                    land.at[q, pl.ds(16, 80), :],
                    send_sem.at[5],
                    recv_sem.at[5],
                    device_id=(p, other),
                    device_id_type=MESH,
                ).start()

            @pl.when(other == q)
            def _():
                pltpu.make_async_copy(
                    slab.at[other], land.at[q, pl.ds(16, 80), :], recv_sem.at[5]
                ).start()

            pltpu.make_async_remote_copy(
                slab.at[other, pl.ds(64, 16), :],
                land.at[q, pl.ds(0, 16), :],
                send_sem.at[5],
                recv_sem.at[5],
                device_id=(north, other),
                device_id_type=MESH,
            ).start()
            pltpu.make_async_remote_copy(
                slab.at[other, pl.ds(0, 16), :],
                land.at[q, pl.ds(96, 16), :],
                send_sem.at[5],
                recv_sem.at[5],
                device_id=(south, other),
                device_id_type=MESH,
            ).start()
        return carry

    lax.fori_loop(0, LON // 2, send_lon, 0)
    pltpu.make_async_copy(land, land, recv_sem.at[5]).wait()

    for h in range(7):
        two = land[:, pl.ds(h * 16, 16), :].astype(F32)
        for k in range(2):
            field = two[:, k * 8 : k * 8 + 8, :].reshape(128, 128).T[:WIDE]
            if h == 0:
                field = jnp.where(p == 0, 0.0, field)
            if h == 6:
                field = jnp.where(p == LAT - 1, 0.0, field)
            q_zero[h * 2 + k] = field

    def step(centre, upper, lower, u, v):
        right = pltpu.roll(centre, WIDE - 1, 0)
        left = pltpu.roll(centre, 1, 0)
        along = centre - 0.5 * u * (right - left) + 0.5 * u * u * (right - 2.0 * centre + left)
        return (
            along - 0.5 * v * (upper - lower) + 0.5 * v * v * (upper - 2.0 * centre + lower)
        )

    def first_step(r, carry):
        q_one[r] = step(q_zero[r + 1], q_zero[r + 2], q_zero[r], flow[0, r], flow[1, r])
        return carry

    lax.fori_loop(0, ROWS + 2, first_step, 0)
    q_one[0] = jnp.where(p == 0, 0.0, q_one[0])
    q_one[ROWS + 1] = jnp.where(p == LAT - 1, 0.0, q_one[ROWS + 1])

    def second_step(r, carry):
        new = step(q_one[r + 1], q_one[r + 2], q_one[r], flow[0, r + 1], flow[1, r + 1])
        new = new[LEAD : LEAD + COLS]
        adv[r] = new
        state[pl.ds(r * 5, 5)] = new.astype(BF16).reshape(5, 16, LEV)
        return carry

    lax.fori_loop(0, ROWS, second_step, 0)
    put_adv = pltpu.make_async_copy(adv, advected_hbm, local_sem.at[6])
    put_adv.start()

    def pack(k, carry):
        out_slots[k] = state[pick[k]]
        return carry

    lax.fori_loop(0, 2 * LON, pack, 0)

    def send_out(t, carry):
        other = lax.rem(q + t, LON)
        pltpu.make_async_remote_copy(
            out_slots.at[pl.ds(other * 2, 2)],
            in_slots.at[pl.ds(q * 2, 2)],
            send_sem.at[6],
            recv_sem.at[6],
            device_id=(p, other),
            device_id_type=MESH,
        ).start()
        return carry

    lax.fori_loop(1, LON, send_out, 0)
    pltpu.make_async_copy(
        out_slots.at[pl.ds(q * 2, 2)], in_slots.at[pl.ds(q * 2, 2)], recv_sem.at[6]
    ).start()
    get_in.wait()
    get_mid.wait()
    get_out.wait()
    pltpu.make_async_copy(in_slots, in_slots, recv_sem.at[6]).wait()
    x = in_slots[...].reshape(HID, LEV)
    one = silu(jnp.dot(x, w_in[0], preferred_element_type=F32)).astype(BF16)
    two = silu(jnp.dot(one, w_mid[0], preferred_element_type=F32)).astype(BF16)
    three = jnp.dot(two, w_out[0], preferred_element_type=F32).astype(BF16)
    back_slots[...] = three.reshape(2 * LON, 16, LEV)

    def send_back(t, carry):
        other = lax.rem(q + t, LON)
        pltpu.make_async_remote_copy(
            back_slots.at[pl.ds(other * 2, 2)],
            ret_slots.at[pl.ds(q * 2, 2)],
            send_sem.at[7],
            recv_sem.at[7],
            device_id=(p, other),
            device_id_type=MESH,
        ).start()
        return carry

    lax.fori_loop(1, LON, send_back, 0)
    pltpu.make_async_copy(
        back_slots.at[pl.ds(q * 2, 2)], ret_slots.at[pl.ds(q * 2, 2)], recv_sem.at[7]
    ).start()
    ret_slots[2 * LON] = jnp.zeros((16, LEV), BF16)
    some = pl.ds(0, 2 * LON)
    pltpu.make_async_copy(ret_slots.at[some], ret_slots.at[some], recv_sem.at[7]).wait()

    def unpack(r, carry):
        for k in range(5):
            heat[r, pl.ds(k * 16, 16), :] = ret_slots[place[r * 5 + k]]
        return carry

    lax.fori_loop(0, ROWS, unpack, 0)
    put_heat = pltpu.make_async_copy(heat, heating_hbm, local_sem.at[7])
    put_heat.start()

    sent = pl.ds(0, LAT - 1)
    pltpu.make_async_copy(pay.at[sent], pay.at[sent], send_sem.at[0]).wait()
    sent = pl.ds(0, LON - 1)
    pltpu.make_async_copy(slab.at[sent], slab.at[sent], send_sem.at[5]).wait()
    sent = pl.ds(0, 2 * LON)
    edge_rows = slab.at[pl.ds(0, LON), pl.ds(0, 32), :]
    pltpu.make_async_copy(edge_rows, edge_rows, send_sem.at[5]).wait()
    sent = pl.ds(0, 2 * LON - 2)
    pltpu.make_async_copy(out_slots.at[sent], out_slots.at[sent], send_sem.at[6]).wait()
    pltpu.make_async_copy(back_slots.at[sent], back_slots.at[sent], send_sem.at[7]).wait()
    put_adv.wait()
    put_heat.wait()


def body(
    spectral,
    wavenumber_of_slot,
    filter_strength,
    courant,
    sunlit_blocks,
    sunlit_owner,
    radiation_in,
    radiation_mid,
    radiation_out,
):
    smem = pl.BlockSpec(memory_space=pltpu.SMEM)
    anywhere = pl.BlockSpec(memory_space=pl.ANY)
    dma = pltpu.SemaphoreType.DMA
    return pl.pallas_call(
        kernel,
        out_shape=(
            jax.ShapeDtypeStruct((ROWS, COLS, LEV), F32),
            jax.ShapeDtypeStruct((ROWS, COLS, LEV), BF16),
        ),
        in_specs=[smem] * 4 + [anywhere] * 6,
        out_specs=(anywhere, anywhere),
        scratch_shapes=[
            pltpu.VMEM((ROWS, 2, OWN, DEG), BF16),
            pltpu.VMEM((LAT * 16, DEG), BF16),
            pltpu.VMEM((2, ROWS, COLS, LEV), BF16),
            pltpu.VMEM((1, LEV, HID), BF16),
            pltpu.VMEM((1, HID, HID), BF16),
            pltpu.VMEM((1, HID, LEV), BF16),
            pltpu.VMEM((256, DEG), BF16),
            pltpu.VMEM((LAT, 16, LEV), BF16),
            pltpu.VMEM((LAT, 16, LEV), BF16),
            pltpu.VMEM((LAT * 16, LEV), F32),
            pltpu.VMEM((COLS, NLON), F32),
            pltpu.VMEM((LON // 2, NLON, 256), BF16),
            pltpu.VMEM((DEG, LEV), F32),
            pltpu.VMEM((LON, COLS, LEV), BF16),
            pltpu.VMEM((LON, 112, LEV), BF16),
            pltpu.VMEM((2, COLS, LEV), BF16),
            pltpu.VMEM((2, COLS, LEV), BF16),
            pltpu.VMEM((2, ROWS, 16, LEV), BF16),
            pltpu.VMEM((2, ROWS, 16, LEV), BF16),
            pltpu.VMEM((2, ROWS + 2, WIDE, LEV), F32),
            pltpu.VMEM((ROWS + 4, WIDE, LEV), F32),
            pltpu.VMEM((ROWS + 2, WIDE, LEV), F32),
            pltpu.VMEM((ROWS, COLS, LEV), F32),
            pltpu.VMEM((50, 16, LEV), BF16),
            pltpu.VMEM((2 * LON, 16, LEV), BF16),
            pltpu.VMEM((2 * LON, 16, LEV), BF16),
            pltpu.VMEM((2 * LON, 16, LEV), BF16),
            pltpu.VMEM((2 * LON + 1, 16, LEV), BF16),
            pltpu.VMEM((ROWS, COLS, LEV), BF16),
            pltpu.SMEM((32,), jnp.int32),
            pltpu.SMEM((50,), jnp.int32),
            dma((8,)),
            dma((8,)),
            dma((8,)),
        ],
        compiler_params=pltpu.CompilerParams(
            collective_id=1, has_side_effects=True, vmem_limit_bytes=48 * 1024 * 1024
        ),
        name="spectral_radiation",
    )(
        wavenumber_of_slot,
        filter_strength,
        sunlit_blocks.reshape(-1),
        sunlit_owner.reshape(-1),
        spectral,
        jnp.asarray(latitude_rows()),
        courant,
        radiation_in,
        radiation_mid,
        radiation_out,
    )


def solution(mesh):
    in_specs = (
        P("lat", None, "lon", None),
        P(),
        P("lon"),
        P(None, "lat", "lon", None),
        P("lat", "lon", None),
        P("lat", "lon", None, None),
        P("lon", None, None),
        P("lon", None, None),
        P("lon", None, None),
    )
    out_specs = (P("lat", "lon", None), P("lat", "lon", None))
    return jax.shard_map(body, mesh=mesh, in_specs=in_specs, out_specs=out_specs, check_vma=False)
```

```python
import math

import jax
import jax.numpy as jnp
import numpy as np
from jax import lax
from jax.experimental import pallas as pl
from jax.experimental.pallas import tpu as pltpu
from jax.sharding import PartitionSpec as P

MESH = pl.DeviceIdType.MESH
F32 = jnp.float32
BF16 = jnp.bfloat16

DEG = 640
NLON = 1280
LAT = 64
LON = 16
ROWS = 10
COLS = 80
LEV = 128
OWN = 8
LEAD = 8
WIDE = 96
HID = 512


def latitude_rows():
    row = np.arange(LAT * 16) % 16
    j = np.arange(LAT * 16) // 16 * ROWS + np.where(row < ROWS, row, row - ROWS)
    n = np.arange(DEG)
    phase = (n[None, :] * (2 * j[:, None] + 1)) % (4 * DEG)
    table = np.cos(phase * (math.pi / (2.0 * DEG))) * math.sqrt(2.0 / DEG)
    return table.astype(np.float32).astype(jnp.bfloat16)


def circle(turns):
    y = turns * math.pi
    z = y * y
    s = 1.0
    for k in (11, 9, 7, 5, 3):
        s = 1.0 - z * s * (1.0 / (k * (k - 1)))
    s = s * y
    c = 1.0
    for k in (12, 10, 8, 6, 4, 2):
        c = 1.0 - z * c * (1.0 / (k * (k - 1)))
    return 1.0 - 2.0 * s * s, 2.0 * s * c


def fraction(product):
    turns = product * (1.0 / NLON)
    return turns - jnp.floor(turns + 0.5)


def silu(v):
    half = 0.5 * v
    return half + half * jnp.tanh(half)


def rank_at(t, p):
    z, k = p // 2, t // 4
    low = jnp.minimum(z, 16)
    down = jnp.where(k < low, low - k, k + 1)
    first = jnp.where(z > 16, 32 - z, 1)
    up = jnp.where(first + k < 16, first + k, 15 - k)
    chip = lax.rem(z + jnp.where(lax.rem(t // 2, 2) == 0, 32 - down, up), 32)
    own = t == LAT - 2
    core = jnp.where(own, 1 - lax.rem(p, 2), lax.rem(t, 2))
    return jnp.where(own, z, chip) * 2 + core


def kernel(
    wave_ref,
    strength_ref,
    sunlit_ref,
    owner_ref,
    spectral_hbm,
    table_hbm,
    courant_hbm,
    win_hbm,
    wmid_hbm,
    wout_hbm,
    advected_hbm,
    heating_hbm,
    spec,
    table,
    cour,
    w_in,
    w_mid,
    w_out,
    damp,
    pay,
    got,
    gotf,
    wide,
    wide_low,
    trig,
    mcol,
    slab,
    land,
    land_south,
    land_north,
    c_north,
    c_south,
    c_west,
    c_east,
    flow,
    q_zero,
    q_one,
    adv,
    state,
    out_slots,
    in_slots,
    back_slots,
    ret_slots,
    heat,
    pick,
    place,
    local_sem,
    send_sem,
    recv_sem,
):
    p = lax.axis_index("lat")
    q = lax.axis_index("lon")
    north = lax.rem(p + 1, LAT)
    south = lax.rem(p + LAT - 1, LAT)
    east = lax.rem(q + 1, LON)
    west = lax.rem(q + LON - 1, LON)

    get_spec = pltpu.make_async_copy(spectral_hbm, spec, local_sem.at[0])
    get_table = pltpu.make_async_copy(table_hbm, table, local_sem.at[1])
    get_cour = pltpu.make_async_copy(courant_hbm, cour, local_sem.at[2])
    get_in = pltpu.make_async_copy(win_hbm, w_in, local_sem.at[3])
    get_mid = pltpu.make_async_copy(wmid_hbm, w_mid, local_sem.at[4])
    get_out = pltpu.make_async_copy(wout_hbm, w_out, local_sem.at[5])
    get_spec.start()
    get_table.start()

    barrier = pltpu.get_barrier_semaphore()

    def greet_lat(t, carry):
        pl.semaphore_signal(barrier, inc=1, device_id=(rank_at(t, p), q), device_id_type=MESH)
        return carry

    lax.fori_loop(0, LAT - 1, greet_lat, 0)

    def greet_lon(t, carry):
        other = lax.rem(q + t, LON)
        pl.semaphore_signal(barrier, inc=1, device_id=(p, other), device_id_type=MESH)
        return carry

    lax.fori_loop(1, LON, greet_lon, 0)

    get_cour.start()
    get_in.start()
    get_mid.start()
    get_out.start()

    degree = lax.broadcasted_iota(jnp.int32, (OWN, DEG), 1)
    level = lax.broadcasted_iota(jnp.int32, (OWN, DEG), 0)
    strength = jnp.zeros((OWN, DEG), F32)
    for l in range(OWN):
        strength = jnp.where(level == l, strength_ref[l], strength)
    relative = (degree * (degree + 1)).astype(F32) / float(DEG * (DEG + 1))
    factor = 1.0 / (1.0 + strength * relative * relative)
    get_spec.wait()
    for s in range(ROWS):
        wave = wave_ref[p * ROWS + s]
        real = jnp.where(degree >= wave, spec[s, 0].astype(F32) * factor, 0.0)
        imag = jnp.where(
            degree >= jnp.where(wave > 0, wave, DEG), spec[s, 1].astype(F32) * factor, 0.0
        )
        both = jnp.concatenate([real, imag], axis=0).astype(BF16)
        damp[pl.ds(s * 16, 16), :] = both
        if s >= 8:
            damp[pl.ds(s * 16 + 32, 16), :] = both
    damp[pl.ds(192, 64), :] = jnp.zeros((64, DEG), BF16)

    get_table.wait()
    row16 = lax.broadcasted_iota(jnp.int32, (128, LEV), 0) % 16
    lane = lax.broadcasted_iota(jnp.int32, (128, LEV), 1)

    def over_degrees(t, carry):
        rows = table[pl.ds(pl.multiple_of(t * 128, 128), 128), :]
        y = lax.dot_general(rows, damp[...], (((1,), (1,)), ((), ())), preferred_element_type=F32)
        first, last = y[:, :128], y[:, 128:]
        tail = jnp.where(lane < 32, last, pltpu.roll(last, 6, 0))
        packed = jnp.where(row16 < ROWS, first, tail).astype(BF16)
        pay[pl.ds(t * 8, 8)] = packed.reshape(8, 16, LEV)
        return carry

    lax.fori_loop(0, 8, over_degrees, 0)

    get_cour.wait()
    pl.semaphore_wait(barrier, LAT + LON - 2)

    edge_north = pltpu.make_async_remote_copy(
        cour.at[:, ROWS - 1],
        c_south,
        send_sem.at[1],
        recv_sem.at[1],
        device_id=(north, q),
        device_id_type=MESH,
    )
    edge_south = pltpu.make_async_remote_copy(
        cour.at[:, 0],
        c_north,
        send_sem.at[2],
        recv_sem.at[2],
        device_id=(south, q),
        device_id_type=MESH,
    )
    edge_east = pltpu.make_async_remote_copy(
        cour.at[:, :, pl.ds(COLS - 16, 16), :],
        c_west,
        send_sem.at[3],
        recv_sem.at[3],
        device_id=(p, east),
        device_id_type=MESH,
    )
    edge_west = pltpu.make_async_remote_copy(
        cour.at[:, :, pl.ds(0, 16), :],
        c_east,
        send_sem.at[4],
        recv_sem.at[4],
        device_id=(p, west),
        device_id_type=MESH,
    )
    edge_east.start()
    edge_west.start()

    @pl.when(p < LAT - 1)
    def _():
        edge_north.start()

    @pl.when(p > 0)
    def _():
        edge_south.start()

    def send_lat(t, carry):
        other = rank_at(t, p)
        pltpu.make_async_remote_copy(
            pay.at[other],
            got.at[p],
            send_sem.at[0],
            recv_sem.at[0],
            device_id=(other, q),
            device_id_type=MESH,
        ).start()
        return carry

    lax.fori_loop(0, LAT - 1, send_lat, 0)
    pltpu.make_async_copy(pay.at[p], got.at[p], recv_sem.at[0]).start()

    sub8 = lax.broadcasted_iota(jnp.int32, (8, LEV), 0)

    def columns(t, carry):
        s, group = t // 8, lax.rem(t, 8)
        value = jnp.zeros((8, LEV), jnp.int32)
        for r in range(8):
            value = jnp.where(sub8 == r, wave_ref[(group * 8 + r) * ROWS + s], value)
        mcol[pl.ds(pl.multiple_of(t * 8, 8), 8), :] = value.astype(F32)
        return carry

    lax.fori_loop(0, 80, columns, 0)

    shift = (lax.broadcasted_iota(jnp.int32, (64, LEV), 1) - LEAD).astype(F32)
    scale = 1.0 / math.sqrt(DEG)

    def trig_rows(s, carry):
        m = mcol[pl.ds(pl.multiple_of(s * 64, 64), 64), :]
        c, d = circle(fraction(m * shift))
        c, d = c * scale, d * scale
        c1, d1 = circle(fraction(m * float(COLS)))
        base = pl.multiple_of(s * 128, 128)
        for other in range(LON):
            lanes = pl.ds((other % 4) * 128, 128)
            trig[other // 4, pl.ds(base, 64), lanes] = c.astype(BF16)
            trig[other // 4, pl.ds(base + 64, 64), lanes] = (-d).astype(BF16)
            c, d = c * c1 - d * d1, d * c1 + c * d1
        return carry

    lax.fori_loop(0, ROWS, trig_rows, 0)

    owners = [owner_ref[t] for t in range(12)]
    listed = [sunlit_ref[t] for t in range(12)]
    slots = []
    for t in range(12):
        rank = jnp.int32(0)
        for u in range(t):
            rank = rank + (owners[u] == owners[t]).astype(jnp.int32)
        slots.append(owners[t] * 2 + rank)

    def fill_pick(k, carry):
        value = jnp.int32(0)
        for t in range(12):
            value = jnp.where(slots[t] == k, listed[t], value)
        pick[k] = value
        return carry

    lax.fori_loop(0, 32, fill_pick, 0)

    def fill_place(k, carry):
        value = jnp.int32(32)
        for t in range(12):
            value = jnp.where(listed[t] == k, slots[t], value)
        place[k] = value
        return carry

    lax.fori_loop(0, 50, fill_place, 0)

    edge_east.wait()
    edge_west.wait()
    zeros8 = jnp.zeros((8, LEV), F32)

    def edge_row(at, edge):
        for k in range(2):
            flow[k, at] = jnp.concatenate([zeros8, edge[k].astype(F32), zeros8], axis=0)

    def fill_flow(r, carry):
        for k in range(2):
            flow[k, r + 1] = jnp.concatenate(
                [
                    c_west[k, r].astype(F32)[8:],
                    cour[k, r].astype(F32),
                    c_east[k, r].astype(F32)[:8],
                ],
                axis=0,
            )
        return carry

    lax.fori_loop(0, ROWS, fill_flow, 0)

    pltpu.make_async_copy(got, got, recv_sem.at[0]).wait()
    gotf[...] = got[...].astype(F32).reshape(LAT * 16, LEV)
    low = lax.broadcasted_iota(jnp.int32, (8, LEV), 1) < 64
    for r in range(16):
        part = gotf[pl.ds(r, LAT, stride=16), :]
        turned = jnp.concatenate([part, part], axis=0).T
        if r < ROWS:
            for a in range(8):
                wide[pl.ds(r * 8, 8), pl.ds(a * 128, 128)] = jnp.where(
                    low, turned[a * 16 : a * 16 + 8], turned[a * 16 + 8 : a * 16 + 16]
                )
        else:
            for g, jj in ((0, r - ROWS), (1, r - ROWS + 4)):
                if g == 1 and jj < 6:
                    continue
                for a in range(2):
                    at = g * 32 + a * 16
                    wide[pl.ds(jj * 8, 8), pl.ds((8 + a) * 128, 128)] = jnp.where(
                        low, turned[at : at + 8], turned[at + 8 : at + 16]
                    )

    wide_low[...] = wide[...].astype(BF16)

    def send_lon(t, carry):
        four = lax.rem(q // 4 + t, LON // 4)
        g = jnp.dot(wide_low[...], trig[four], preferred_element_type=F32).astype(BF16)
        for h in range(4):
            other = four * 4 + h
            slab[other] = g[:, h * 128 : (h + 1) * 128]

            @pl.when(other != q)
            def _():
                pltpu.make_async_remote_copy(
                    slab.at[other],
                    land.at[q],
                    send_sem.at[5],
                    recv_sem.at[5],
                    device_id=(p, other),
                    device_id_type=MESH,
                ).start()

            @pl.when(other == q)
            def _():
                pltpu.make_async_copy(
                    slab.at[other], land.at[q], recv_sem.at[5]
                ).start()

            @pl.when(p < LAT - 1)
            def _():
                pltpu.make_async_remote_copy(
                    slab.at[other, pl.ds(64, 16), :],
                    land_south.at[q],
                    send_sem.at[8],
                    recv_sem.at[8],
                    device_id=(north, other),
                    device_id_type=MESH,
                ).start()

            @pl.when(p > 0)
            def _():
                pltpu.make_async_remote_copy(
                    slab.at[other, pl.ds(0, 16), :],
                    land_north.at[q],
                    send_sem.at[9],
                    recv_sem.at[9],
                    device_id=(south, other),
                    device_id_type=MESH,
                ).start()

        return carry

    lax.fori_loop(0, LON // 4, send_lon, 0)
    def assemble(two, at):
        for k in range(2):
            q_zero[at + k] = two[:, k * 8 : k * 8 + 8, :].reshape(128, 128).T[:WIDE]

    pltpu.make_async_copy(land, land, recv_sem.at[5]).wait()
    for h in range(5):
        assemble(land[:, pl.ds(h * 16, 16), :].astype(F32), 2 + h * 2)

    @pl.when(p > 0)
    def _():
        pltpu.make_async_copy(land_south, land_south, recv_sem.at[8]).wait()
        assemble(land_south[...].astype(F32), 0)
        edge_south.wait_send()
        edge_north.wait_recv()
        edge_row(0, c_south)

    @pl.when(p == 0)
    def _():
        q_zero[pl.ds(0, 2)] = jnp.zeros((2, WIDE, LEV), F32)
        flow[0, 0] = jnp.zeros((WIDE, LEV), F32)
        flow[1, 0] = jnp.zeros((WIDE, LEV), F32)

    @pl.when(p < LAT - 1)
    def _():
        pltpu.make_async_copy(land_north, land_north, recv_sem.at[9]).wait()
        assemble(land_north[...].astype(F32), ROWS + 2)
        edge_north.wait_send()
        edge_south.wait_recv()
        edge_row(ROWS + 1, c_north)

    @pl.when(p == LAT - 1)
    def _():
        q_zero[pl.ds(ROWS + 2, 2)] = jnp.zeros((2, WIDE, LEV), F32)
        flow[0, ROWS + 1] = jnp.zeros((WIDE, LEV), F32)
        flow[1, ROWS + 1] = jnp.zeros((WIDE, LEV), F32)

    def step(centre, upper, lower, u, v):
        right = pltpu.roll(centre, WIDE - 1, 0)
        left = pltpu.roll(centre, 1, 0)
        along = centre - 0.5 * u * (right - left) + 0.5 * u * u * (right - 2.0 * centre + left)
        return (
            along - 0.5 * v * (upper - lower) + 0.5 * v * v * (upper - 2.0 * centre + lower)
        )

    def first_step(r, carry):
        q_one[r] = step(q_zero[r + 1], q_zero[r + 2], q_zero[r], flow[0, r], flow[1, r])
        return carry

    lax.fori_loop(0, ROWS + 2, first_step, 0)
    q_one[0] = jnp.where(p == 0, 0.0, q_one[0])
    q_one[ROWS + 1] = jnp.where(p == LAT - 1, 0.0, q_one[ROWS + 1])

    def second_step(r, carry):
        new = step(q_one[r + 1], q_one[r + 2], q_one[r], flow[0, r + 1], flow[1, r + 1])
        new = new[LEAD : LEAD + COLS]
        adv[r] = new
        state[pl.ds(r * 5, 5)] = new.astype(BF16).reshape(5, 16, LEV)
        return carry

    lax.fori_loop(0, ROWS, second_step, 0)
    put_adv = pltpu.make_async_copy(adv, advected_hbm, local_sem.at[6])
    put_adv.start()

    def pack(k, carry):
        out_slots[k] = state[pick[k]]
        return carry

    lax.fori_loop(0, 2 * LON, pack, 0)

    def send_out(t, carry):
        other = lax.rem(q + t, LON)
        pltpu.make_async_remote_copy(
            out_slots.at[pl.ds(other * 2, 2)],
            in_slots.at[pl.ds(q * 2, 2)],
            send_sem.at[6],
            recv_sem.at[6],
            device_id=(p, other),
            device_id_type=MESH,
        ).start()
        return carry

    lax.fori_loop(1, LON, send_out, 0)
    pltpu.make_async_copy(
        out_slots.at[pl.ds(q * 2, 2)], in_slots.at[pl.ds(q * 2, 2)], recv_sem.at[6]
    ).start()
    get_in.wait()
    get_mid.wait()
    get_out.wait()
    pltpu.make_async_copy(in_slots, in_slots, recv_sem.at[6]).wait()
    x = in_slots[...].reshape(HID, LEV)
    one = silu(jnp.dot(x, w_in[0], preferred_element_type=F32)).astype(BF16)
    two = silu(jnp.dot(one, w_mid[0], preferred_element_type=F32)).astype(BF16)
    three = jnp.dot(two, w_out[0], preferred_element_type=F32).astype(BF16)
    back_slots[...] = three.reshape(2 * LON, 16, LEV)

    def send_back(t, carry):
        other = lax.rem(q + t, LON)
        pltpu.make_async_remote_copy(
            back_slots.at[pl.ds(other * 2, 2)],
            ret_slots.at[pl.ds(q * 2, 2)],
            send_sem.at[7],
            recv_sem.at[7],
            device_id=(p, other),
            device_id_type=MESH,
        ).start()
        return carry

    lax.fori_loop(1, LON, send_back, 0)
    pltpu.make_async_copy(
        back_slots.at[pl.ds(q * 2, 2)], ret_slots.at[pl.ds(q * 2, 2)], recv_sem.at[7]
    ).start()
    ret_slots[2 * LON] = jnp.zeros((16, LEV), BF16)
    some = pl.ds(0, 2 * LON)
    pltpu.make_async_copy(ret_slots.at[some], ret_slots.at[some], recv_sem.at[7]).wait()

    def unpack(r, carry):
        for k in range(5):
            heat[r, pl.ds(k * 16, 16), :] = ret_slots[place[r * 5 + k]]
        return carry

    lax.fori_loop(0, ROWS, unpack, 0)
    put_heat = pltpu.make_async_copy(heat, heating_hbm, local_sem.at[7])
    put_heat.start()

    sent = pl.ds(0, LAT - 1)
    pltpu.make_async_copy(pay.at[sent], pay.at[sent], send_sem.at[0]).wait()
    sent = pl.ds(0, LON - 1)
    pltpu.make_async_copy(slab.at[sent], slab.at[sent], send_sem.at[5]).wait()

    @pl.when(p < LAT - 1)
    def _():
        pltpu.make_async_copy(land_south, land_south, send_sem.at[8]).wait()

    @pl.when(p > 0)
    def _():
        pltpu.make_async_copy(land_north, land_north, send_sem.at[9]).wait()

    sent = pl.ds(0, 2 * LON - 2)
    pltpu.make_async_copy(out_slots.at[sent], out_slots.at[sent], send_sem.at[6]).wait()
    pltpu.make_async_copy(back_slots.at[sent], back_slots.at[sent], send_sem.at[7]).wait()
    put_adv.wait()
    put_heat.wait()


def body(
    spectral,
    wavenumber_of_slot,
    filter_strength,
    courant,
    sunlit_blocks,
    sunlit_owner,
    radiation_in,
    radiation_mid,
    radiation_out,
):
    smem = pl.BlockSpec(memory_space=pltpu.SMEM)
    anywhere = pl.BlockSpec(memory_space=pl.ANY)
    dma = pltpu.SemaphoreType.DMA
    return pl.pallas_call(
        kernel,
        out_shape=(
            jax.ShapeDtypeStruct((ROWS, COLS, LEV), F32),
            jax.ShapeDtypeStruct((ROWS, COLS, LEV), BF16),
        ),
        in_specs=[smem] * 4 + [anywhere] * 6,
        out_specs=(anywhere, anywhere),
        scratch_shapes=[
            pltpu.VMEM((ROWS, 2, OWN, DEG), BF16),
            pltpu.VMEM((LAT * 16, DEG), BF16),
            pltpu.VMEM((2, ROWS, COLS, LEV), BF16),
            pltpu.VMEM((1, LEV, HID), BF16),
            pltpu.VMEM((1, HID, HID), BF16),
            pltpu.VMEM((1, HID, LEV), BF16),
            pltpu.VMEM((256, DEG), BF16),
            pltpu.VMEM((LAT, 16, LEV), BF16),
            pltpu.VMEM((LAT, 16, LEV), BF16),
            pltpu.VMEM((LAT * 16, LEV), F32),
            pltpu.VMEM((COLS, NLON), F32),
            pltpu.VMEM((COLS, NLON), BF16),
            pltpu.VMEM((LON // 4, NLON, 512), BF16),
            pltpu.VMEM((DEG, LEV), F32),
            pltpu.VMEM((LON, COLS, LEV), BF16),
            pltpu.VMEM((LON, COLS, LEV), BF16),
            pltpu.VMEM((LON, 16, LEV), BF16),
            pltpu.VMEM((LON, 16, LEV), BF16),
            pltpu.VMEM((2, COLS, LEV), BF16),
            pltpu.VMEM((2, COLS, LEV), BF16),
            pltpu.VMEM((2, ROWS, 16, LEV), BF16),
            pltpu.VMEM((2, ROWS, 16, LEV), BF16),
            pltpu.VMEM((2, ROWS + 2, WIDE, LEV), F32),
            pltpu.VMEM((ROWS + 4, WIDE, LEV), F32),
            pltpu.VMEM((ROWS + 2, WIDE, LEV), F32),
            pltpu.VMEM((ROWS, COLS, LEV), F32),
            pltpu.VMEM((50, 16, LEV), BF16),
            pltpu.VMEM((2 * LON, 16, LEV), BF16),
            pltpu.VMEM((2 * LON, 16, LEV), BF16),
            pltpu.VMEM((2 * LON, 16, LEV), BF16),
            pltpu.VMEM((2 * LON + 1, 16, LEV), BF16),
            pltpu.VMEM((ROWS, COLS, LEV), BF16),
            pltpu.SMEM((32,), jnp.int32),
            pltpu.SMEM((50,), jnp.int32),
            dma((8,)),
            dma((10,)),
            dma((10,)),
        ],
        compiler_params=pltpu.CompilerParams(
            collective_id=1, has_side_effects=True, vmem_limit_bytes=64 * 1024 * 1024
        ),
        name="spectral_radiation",
    )(
        wavenumber_of_slot,
        filter_strength,
        sunlit_blocks.reshape(-1),
        sunlit_owner.reshape(-1),
        spectral,
        jnp.asarray(latitude_rows()),
        courant,
        radiation_in,
        radiation_mid,
        radiation_out,
    )


def solution(mesh):
    in_specs = (
        P("lat", None, "lon", None),
        P(),
        P("lon"),
        P(None, "lat", "lon", None),
        P("lat", "lon", None),
        P("lat", "lon", None, None),
        P("lon", None, None),
        P("lon", None, None),
        P("lon", None, None),
    )
    out_specs = (P("lat", "lon", None), P("lat", "lon", None))
    return jax.shard_map(body, mesh=mesh, in_specs=in_specs, out_specs=out_specs, check_vma=False)
```

```python
import functools
import math

import jax
import jax.numpy as jnp
import numpy as np
from jax import lax
from jax.experimental import pallas as pl
from jax.experimental.pallas import tpu as pltpu
from jax.sharding import PartitionSpec as P

MESH = pl.DeviceIdType.MESH
F32 = jnp.float32
BF16 = jnp.bfloat16

DEG = 640
NLON = 1280
LAT = 64
LON = 16
ROWS = 10
COLS = 80
LEV = 128
OWN = 8
LEAD = 8
WIDE = 96
HID = 512
PACK = 14


def latitude_rows():
    row = np.arange(LAT * 16) % 16
    j = np.arange(LAT * 16) // 16 * ROWS + np.where(row < ROWS, row, row - ROWS)
    n = np.arange(DEG)
    phase = (n[None, :] * (2 * j[:, None] + 1)) % (4 * DEG)
    table = np.cos(phase * (math.pi / (2.0 * DEG))) * math.sqrt(2.0 / DEG)
    return table.astype(np.float32).astype(jnp.bfloat16)


def circle(turns):
    y = turns * math.pi
    z = y * y
    s = 1.0
    for k in (11, 9, 7, 5, 3):
        s = 1.0 - z * s * (1.0 / (k * (k - 1)))
    s = s * y
    c = 1.0
    for k in (12, 10, 8, 6, 4, 2):
        c = 1.0 - z * c * (1.0 / (k * (k - 1)))
    return 1.0 - 2.0 * s * s, 2.0 * s * c


def fraction(product):
    turns = product * (1.0 / NLON)
    return turns - jnp.floor(turns + 0.5)


def silu(v):
    half = 0.5 * v
    return half + half * jnp.tanh(half)


REACH = 8
NEAR = 4 * REACH + 1
FAR = LAT - 1 - NEAR


def rank_at(t, p, least, down_most, up_most):
    z, k = p // 2, t // 4
    low = jnp.minimum(z, down_most)
    down = jnp.where(k < low - least + 1, low - k, least + k)
    first = jnp.where(z > 31 - up_most, jnp.maximum(32 - z, least), least)
    up = jnp.where(first + k <= up_most, first + k, up_most - k)
    chip = lax.rem(z + jnp.where(lax.rem(t // 2, 2) == 0, 32 - down, up), 32)
    return chip * 2 + lax.rem(t, 2)


def near_rank(t, p):
    other = rank_at(t, p, 1, REACH, REACH)
    return jnp.where(t == NEAR - 1, p + 1 - 2 * lax.rem(p, 2), other)


def far_rank(t, p):
    return rank_at(t, p, REACH + 1, 16, 15)


def kernel(
    wave_ref,
    strength_ref,
    sunlit_ref,
    owner_ref,
    spectral_hbm,
    table_hbm,
    courant_hbm,
    win_hbm,
    wmid_hbm,
    wout_hbm,
    advected_hbm,
    heating_hbm,
    spec,
    table,
    cour,
    w_in,
    w_mid,
    w_out,
    damp,
    pay,
    got,
    gotf,
    wide,
    wide_low,
    trig,
    mcol,
    slab,
    land,
    land_south,
    land_north,
    c_north,
    c_south,
    c_west,
    c_east,
    flow,
    q_zero,
    q_one,
    adv,
    state,
    out_slots,
    in_slots,
    back_slots,
    ret_slots,
    heat,
    pick,
    place,
    local_sem,
    send_sem,
    recv_sem,
    heard,
):
    p = lax.axis_index("lat")
    q = lax.axis_index("lon")
    north = lax.rem(p + 1, LAT)
    south = lax.rem(p + LAT - 1, LAT)
    east = lax.rem(q + 1, LON)
    west = lax.rem(q + LON - 1, LON)

    get_spec = pltpu.make_async_copy(spectral_hbm, spec, local_sem.at[0])
    get_table = pltpu.make_async_copy(table_hbm, table, local_sem.at[1])
    get_cour = pltpu.make_async_copy(courant_hbm, cour, local_sem.at[2])
    get_in = pltpu.make_async_copy(win_hbm, w_in, local_sem.at[3])
    get_mid = pltpu.make_async_copy(wmid_hbm, w_mid, local_sem.at[4])
    get_out = pltpu.make_async_copy(wout_hbm, w_out, local_sem.at[5])
    get_spec.start()
    get_table.start()

    barrier = pltpu.get_barrier_semaphore()

    def greet_lat(t, carry):
        pl.semaphore_signal(barrier, inc=1, device_id=(near_rank(t, p), q), device_id_type=MESH)
        return carry

    lax.fori_loop(0, NEAR, greet_lat, 0)

    def greet_lon(t, carry):
        other = lax.rem(q + t, LON)
        pl.semaphore_signal(barrier, inc=1, device_id=(p, other), device_id_type=MESH)
        return carry

    lax.fori_loop(1, LON, greet_lon, 0)

    get_cour.start()
    get_in.start()
    get_mid.start()
    get_out.start()

    degree = lax.broadcasted_iota(jnp.int32, (OWN, DEG), 1)
    level = lax.broadcasted_iota(jnp.int32, (OWN, DEG), 0)
    strength = jnp.zeros((OWN, DEG), F32)
    for l in range(OWN):
        strength = jnp.where(level == l, strength_ref[l], strength)
    relative = (degree * (degree + 1)).astype(F32) / float(DEG * (DEG + 1))
    factor = 1.0 / (1.0 + strength * relative * relative)
    get_spec.wait()
    for s in range(ROWS):
        wave = wave_ref[p * ROWS + s]
        real = jnp.where(degree >= wave, spec[s, 0].astype(F32) * factor, 0.0)
        imag = jnp.where(
            degree >= jnp.where(wave > 0, wave, DEG), spec[s, 1].astype(F32) * factor, 0.0
        )
        both = jnp.concatenate([real, imag], axis=0).astype(BF16)
        damp[pl.ds(s * 16, 16), :] = both
        if s >= 8:
            damp[pl.ds(s * 16 + 32, 16), :] = both
            damp[pl.ds(s * 16 + 64, 16), :] = both
    damp[pl.ds(224, 32), :] = jnp.zeros((32, DEG), BF16)

    get_table.wait()
    row16 = lax.broadcasted_iota(jnp.int32, (LAT * 16, LEV), 0) % 16
    lane = lax.broadcasted_iota(jnp.int32, (LAT * 16, LEV), 1)
    y = lax.dot_general(
        table[...], damp[...], (((1,), (1,)), ((), ())), preferred_element_type=F32
    )
    first, last = y[:, :128], y[:, 128:]
    tail = jnp.where(
        lane < 32, last, jnp.where(lane < 64, pltpu.roll(last, 6, 0), pltpu.roll(last, 2, 0))
    )
    packed = jnp.where(row16 < ROWS, first, tail).astype(BF16)
    pay[...] = packed.reshape(LAT, 8, 2, LEV)[:, : PACK // 2]

    get_cour.wait()
    pl.semaphore_wait(barrier, NEAR + LON - 1)
    for d in (REACH, 32 - REACH):
        pl.semaphore_signal(
            heard, inc=1, device_id=(lax.rem(p + 2 * d, LAT), q), device_id_type=MESH
        )

    edge_north = pltpu.make_async_remote_copy(
        cour.at[:, ROWS - 1],
        c_south,
        send_sem.at[1],
        recv_sem.at[1],
        device_id=(north, q),
        device_id_type=MESH,
    )
    edge_south = pltpu.make_async_remote_copy(
        cour.at[:, 0],
        c_north,
        send_sem.at[2],
        recv_sem.at[2],
        device_id=(south, q),
        device_id_type=MESH,
    )
    edge_east = pltpu.make_async_remote_copy(
        cour.at[:, :, pl.ds(COLS - 16, 16), :],
        c_west,
        send_sem.at[3],
        recv_sem.at[3],
        device_id=(p, east),
        device_id_type=MESH,
    )
    edge_west = pltpu.make_async_remote_copy(
        cour.at[:, :, pl.ds(0, 16), :],
        c_east,
        send_sem.at[4],
        recv_sem.at[4],
        device_id=(p, west),
        device_id_type=MESH,
    )
    def send_lat(rank_of, t, carry):
        other = rank_of(t, p)
        pltpu.make_async_remote_copy(
            pay.at[other],
            got.at[p],
            send_sem.at[0],
            recv_sem.at[0],
            device_id=(other, q),
            device_id_type=MESH,
        ).start()
        return carry

    lax.fori_loop(0, NEAR, functools.partial(send_lat, near_rank), 0)
    pltpu.make_async_copy(pay.at[p], got.at[p], recv_sem.at[0]).start()

    edge_east.start()
    edge_west.start()

    sub8 = lax.broadcasted_iota(jnp.int32, (8, LEV), 0)

    def columns(t, carry):
        s, group = t // 8, lax.rem(t, 8)
        value = jnp.zeros((8, LEV), jnp.int32)
        for r in range(8):
            value = jnp.where(sub8 == r, wave_ref[(group * 8 + r) * ROWS + s], value)
        mcol[pl.ds(pl.multiple_of(t * 8, 8), 8), :] = value.astype(F32)
        return carry

    lax.fori_loop(0, 80, columns, 0)

    shift = (lax.broadcasted_iota(jnp.int32, (64, LEV), 1) - LEAD).astype(F32)
    scale = 1.0 / math.sqrt(DEG)

    def trig_rows(s, carry):
        m = mcol[pl.ds(pl.multiple_of(s * 64, 64), 64), :]
        c, d = circle(fraction(m * shift))
        c, d = c * scale, d * scale
        c1, d1 = circle(fraction(m * float(COLS)))
        base = pl.multiple_of(s * 128, 128)
        for other in range(LON):
            lanes = pl.ds((other % 4) * 128, 128)
            trig[other // 4, pl.ds(base, 64), lanes] = c.astype(BF16)
            trig[other // 4, pl.ds(base + 64, 64), lanes] = (-d).astype(BF16)
            c, d = c * c1 - d * d1, d * c1 + c * d1
        return carry

    lax.fori_loop(0, ROWS, trig_rows, 0)

    pl.semaphore_wait(heard, 2)
    lax.fori_loop(0, FAR, functools.partial(send_lat, far_rank), 0)
    @pl.when(p < LAT - 1)
    def _():
        edge_north.start()

    @pl.when(p > 0)
    def _():
        edge_south.start()

    owners = [owner_ref[t] for t in range(12)]
    listed = [sunlit_ref[t] for t in range(12)]
    slots = []
    for t in range(12):
        rank = jnp.int32(0)
        for u in range(t):
            rank = rank + (owners[u] == owners[t]).astype(jnp.int32)
        slots.append(owners[t] * 2 + rank)

    def fill_pick(k, carry):
        value = jnp.int32(0)
        for t in range(12):
            value = jnp.where(slots[t] == k, listed[t], value)
        pick[k] = value
        return carry

    lax.fori_loop(0, 32, fill_pick, 0)

    def fill_place(k, carry):
        value = jnp.int32(32)
        for t in range(12):
            value = jnp.where(listed[t] == k, slots[t], value)
        place[k] = value
        return carry

    lax.fori_loop(0, 50, fill_place, 0)

    edge_east.wait()
    edge_west.wait()
    zeros8 = jnp.zeros((8, LEV), F32)

    def edge_row(at, edge):
        for k in range(2):
            flow[k, at] = jnp.concatenate([zeros8, edge[k].astype(F32), zeros8], axis=0)

    def fill_flow(r, carry):
        for k in range(2):
            flow[k, r + 1] = jnp.concatenate(
                [
                    c_west[k, r].astype(F32)[8:],
                    cour[k, r].astype(F32),
                    c_east[k, r].astype(F32)[:8],
                ],
                axis=0,
            )
        return carry

    lax.fori_loop(0, ROWS, fill_flow, 0)

    pltpu.make_async_copy(got, got, recv_sem.at[0]).wait()
    gotf[...] = got[...].astype(F32).reshape(LAT * PACK, LEV)
    low = lax.broadcasted_iota(jnp.int32, (8, LEV), 1) < 64
    for r in range(PACK):
        part = gotf[pl.ds(r, LAT, stride=PACK), :]
        turned = jnp.concatenate([part, part], axis=0).T
        if r < ROWS:
            for a in range(8):
                wide[pl.ds(r * 8, 8), pl.ds(a * 128, 128)] = jnp.where(
                    low, turned[a * 16 : a * 16 + 8], turned[a * 16 + 8 : a * 16 + 16]
                )
        else:
            for g, jj in enumerate(range(r - ROWS, ROWS, 4)):
                for a in range(2):
                    at = g * 32 + a * 16
                    wide[pl.ds(jj * 8, 8), pl.ds((8 + a) * 128, 128)] = jnp.where(
                        low, turned[at : at + 8], turned[at + 8 : at + 16]
                    )

    wide_low[...] = wide[...].astype(BF16)

    def send_lon(t, carry):
        four = lax.rem(q // 4 + t, LON // 4)
        g = jnp.dot(wide_low[...], trig[four], preferred_element_type=F32).astype(BF16)
        for h in range(4):
            other = four * 4 + h
            slab[other] = g[:, h * 128 : (h + 1) * 128]

            @pl.when(other != q)
            def _():
                pltpu.make_async_remote_copy(
                    slab.at[other],
                    land.at[q],
                    send_sem.at[5],
                    recv_sem.at[5],
                    device_id=(p, other),
                    device_id_type=MESH,
                ).start()

            @pl.when(other == q)
            def _():
                pltpu.make_async_copy(
                    slab.at[other], land.at[q], recv_sem.at[5]
                ).start()

            @pl.when(p < LAT - 1)
            def _():
                pltpu.make_async_remote_copy(
                    slab.at[other, pl.ds(64, 16), :],
                    land_south.at[q],
                    send_sem.at[8],
                    recv_sem.at[8],
                    device_id=(north, other),
                    device_id_type=MESH,
                ).start()

            @pl.when(p > 0)
            def _():
                pltpu.make_async_remote_copy(
                    slab.at[other, pl.ds(0, 16), :],
                    land_north.at[q],
                    send_sem.at[9],
                    recv_sem.at[9],
                    device_id=(south, other),
                    device_id_type=MESH,
                ).start()

        return carry

    lax.fori_loop(0, LON // 4, send_lon, 0)
    def assemble(two, at):
        for k in range(2):
            q_zero[at + k] = two[:, k * 8 : k * 8 + 8, :].reshape(128, 128).T[:WIDE]

    pltpu.make_async_copy(land, land, recv_sem.at[5]).wait()
    for h in range(5):
        assemble(land[:, pl.ds(h * 16, 16), :].astype(F32), 2 + h * 2)

    @pl.when(p > 0)
    def _():
        pltpu.make_async_copy(land_south, land_south, recv_sem.at[8]).wait()
        assemble(land_south[...].astype(F32), 0)
        edge_south.wait_send()
        edge_north.wait_recv()
        edge_row(0, c_south)

    @pl.when(p == 0)
    def _():
        q_zero[pl.ds(0, 2)] = jnp.zeros((2, WIDE, LEV), F32)
        flow[0, 0] = jnp.zeros((WIDE, LEV), F32)
        flow[1, 0] = jnp.zeros((WIDE, LEV), F32)

    @pl.when(p < LAT - 1)
    def _():
        pltpu.make_async_copy(land_north, land_north, recv_sem.at[9]).wait()
        assemble(land_north[...].astype(F32), ROWS + 2)
        edge_north.wait_send()
        edge_south.wait_recv()
        edge_row(ROWS + 1, c_north)

    @pl.when(p == LAT - 1)
    def _():
        q_zero[pl.ds(ROWS + 2, 2)] = jnp.zeros((2, WIDE, LEV), F32)
        flow[0, ROWS + 1] = jnp.zeros((WIDE, LEV), F32)
        flow[1, ROWS + 1] = jnp.zeros((WIDE, LEV), F32)

    def step(centre, upper, lower, u, v):
        right = pltpu.roll(centre, WIDE - 1, 0)
        left = pltpu.roll(centre, 1, 0)
        along = centre - 0.5 * u * (right - left) + 0.5 * u * u * (right - 2.0 * centre + left)
        return (
            along - 0.5 * v * (upper - lower) + 0.5 * v * v * (upper - 2.0 * centre + lower)
        )

    def first_step(r, carry):
        q_one[r] = step(q_zero[r + 1], q_zero[r + 2], q_zero[r], flow[0, r], flow[1, r])
        return carry

    lax.fori_loop(0, ROWS + 2, first_step, 0)
    q_one[0] = jnp.where(p == 0, 0.0, q_one[0])
    q_one[ROWS + 1] = jnp.where(p == LAT - 1, 0.0, q_one[ROWS + 1])

    def second_step(r, carry):
        new = step(q_one[r + 1], q_one[r + 2], q_one[r], flow[0, r + 1], flow[1, r + 1])
        new = new[LEAD : LEAD + COLS]
        adv[r] = new
        state[pl.ds(r * 5, 5)] = new.astype(BF16).reshape(5, 16, LEV)
        return carry

    lax.fori_loop(0, ROWS, second_step, 0)
    put_adv = pltpu.make_async_copy(adv, advected_hbm, local_sem.at[6])
    put_adv.start()

    def pack(other):
        for k in range(2):
            out_slots[other * 2 + k] = state[pick[other * 2 + k]]

    def send_out(t, carry):
        other = lax.rem(q + t, LON)
        pack(other)
        pltpu.make_async_remote_copy(
            out_slots.at[pl.ds(other * 2, 2)],
            in_slots.at[pl.ds(q * 2, 2)],
            send_sem.at[6],
            recv_sem.at[6],
            device_id=(p, other),
            device_id_type=MESH,
        ).start()
        return carry

    lax.fori_loop(1, LON, send_out, 0)
    pack(q)
    pltpu.make_async_copy(
        out_slots.at[pl.ds(q * 2, 2)], in_slots.at[pl.ds(q * 2, 2)], recv_sem.at[6]
    ).start()
    get_in.wait()
    get_mid.wait()
    get_out.wait()
    pltpu.make_async_copy(in_slots, in_slots, recv_sem.at[6]).wait()
    x = in_slots[...].reshape(HID, LEV)
    one = silu(jnp.dot(x, w_in[0], preferred_element_type=F32)).astype(BF16)
    two = silu(jnp.dot(one, w_mid[0], preferred_element_type=F32)).astype(BF16)
    three = jnp.dot(two, w_out[0], preferred_element_type=F32).astype(BF16)
    back_slots[...] = three.reshape(2 * LON, 16, LEV)

    def send_back(t, carry):
        other = lax.rem(q + t, LON)
        pltpu.make_async_remote_copy(
            back_slots.at[pl.ds(other * 2, 2)],
            ret_slots.at[pl.ds(q * 2, 2)],
            send_sem.at[7],
            recv_sem.at[7],
            device_id=(p, other),
            device_id_type=MESH,
        ).start()
        return carry

    lax.fori_loop(1, LON, send_back, 0)
    pltpu.make_async_copy(
        back_slots.at[pl.ds(q * 2, 2)], ret_slots.at[pl.ds(q * 2, 2)], recv_sem.at[7]
    ).start()
    ret_slots[2 * LON] = jnp.zeros((16, LEV), BF16)
    some = pl.ds(0, 2 * LON)
    pltpu.make_async_copy(ret_slots.at[some], ret_slots.at[some], recv_sem.at[7]).wait()

    def unpack(r, carry):
        for k in range(5):
            heat[r, pl.ds(k * 16, 16), :] = ret_slots[place[r * 5 + k]]
        return carry

    lax.fori_loop(0, ROWS, unpack, 0)
    put_heat = pltpu.make_async_copy(heat, heating_hbm, local_sem.at[7])
    put_heat.start()

    sent = pl.ds(0, LAT - 1)
    pltpu.make_async_copy(pay.at[sent], pay.at[sent], send_sem.at[0]).wait()
    sent = pl.ds(0, LON - 1)
    pltpu.make_async_copy(slab.at[sent], slab.at[sent], send_sem.at[5]).wait()

    @pl.when(p < LAT - 1)
    def _():
        pltpu.make_async_copy(land_south, land_south, send_sem.at[8]).wait()

    @pl.when(p > 0)
    def _():
        pltpu.make_async_copy(land_north, land_north, send_sem.at[9]).wait()

    sent = pl.ds(0, 2 * LON - 2)
    pltpu.make_async_copy(out_slots.at[sent], out_slots.at[sent], send_sem.at[6]).wait()
    pltpu.make_async_copy(back_slots.at[sent], back_slots.at[sent], send_sem.at[7]).wait()
    put_adv.wait()
    put_heat.wait()


def body(
    spectral,
    wavenumber_of_slot,
    filter_strength,
    courant,
    sunlit_blocks,
    sunlit_owner,
    radiation_in,
    radiation_mid,
    radiation_out,
):
    smem = pl.BlockSpec(memory_space=pltpu.SMEM)
    anywhere = pl.BlockSpec(memory_space=pl.ANY)
    dma = pltpu.SemaphoreType.DMA
    return pl.pallas_call(
        kernel,
        out_shape=(
            jax.ShapeDtypeStruct((ROWS, COLS, LEV), F32),
            jax.ShapeDtypeStruct((ROWS, COLS, LEV), BF16),
        ),
        in_specs=[smem] * 4 + [anywhere] * 6,
        out_specs=(anywhere, anywhere),
        scratch_shapes=[
            pltpu.VMEM((ROWS, 2, OWN, DEG), BF16),
            pltpu.VMEM((LAT * 16, DEG), BF16),
            pltpu.VMEM((2, ROWS, COLS, LEV), BF16),
            pltpu.VMEM((1, LEV, HID), BF16),
            pltpu.VMEM((1, HID, HID), BF16),
            pltpu.VMEM((1, HID, LEV), BF16),
            pltpu.VMEM((256, DEG), BF16),
            pltpu.VMEM((LAT, PACK // 2, 2, LEV), BF16),
            pltpu.VMEM((LAT, PACK // 2, 2, LEV), BF16),
            pltpu.VMEM((LAT * PACK, LEV), F32),
            pltpu.VMEM((COLS, NLON), F32),
            pltpu.VMEM((COLS, NLON), BF16),
            pltpu.VMEM((LON // 4, NLON, 512), BF16),
            pltpu.VMEM((DEG, LEV), F32),
            pltpu.VMEM((LON, COLS, LEV), BF16),
            pltpu.VMEM((LON, COLS, LEV), BF16),
            pltpu.VMEM((LON, 16, LEV), BF16),
            pltpu.VMEM((LON, 16, LEV), BF16),
            pltpu.VMEM((2, COLS, LEV), BF16),
            pltpu.VMEM((2, COLS, LEV), BF16),
            pltpu.VMEM((2, ROWS, 16, LEV), BF16),
            pltpu.VMEM((2, ROWS, 16, LEV), BF16),
            pltpu.VMEM((2, ROWS + 2, WIDE, LEV), F32),
            pltpu.VMEM((ROWS + 4, WIDE, LEV), F32),
            pltpu.VMEM((ROWS + 2, WIDE, LEV), F32),
            pltpu.VMEM((ROWS, COLS, LEV), F32),
            pltpu.VMEM((50, 16, LEV), BF16),
            pltpu.VMEM((2 * LON, 16, LEV), BF16),
            pltpu.VMEM((2 * LON, 16, LEV), BF16),
            pltpu.VMEM((2 * LON, 16, LEV), BF16),
            pltpu.VMEM((2 * LON + 1, 16, LEV), BF16),
            pltpu.VMEM((ROWS, COLS, LEV), BF16),
            pltpu.SMEM((32,), jnp.int32),
            pltpu.SMEM((50,), jnp.int32),
            dma((8,)),
            dma((10,)),
            dma((10,)),
            pltpu.SemaphoreType.REGULAR,
        ],
        compiler_params=pltpu.CompilerParams(
            collective_id=1, has_side_effects=True, vmem_limit_bytes=64 * 1024 * 1024
        ),
        name="spectral_radiation",
    )(
        wavenumber_of_slot,
        filter_strength,
        sunlit_blocks.reshape(-1),
        sunlit_owner.reshape(-1),
        spectral,
        jnp.asarray(latitude_rows()),
        courant,
        radiation_in,
        radiation_mid,
        radiation_out,
    )


def solution(mesh):
    in_specs = (
        P("lat", None, "lon", None),
        P(),
        P("lon"),
        P(None, "lat", "lon", None),
        P("lat", "lon", None),
        P("lat", "lon", None, None),
        P("lon", None, None),
        P("lon", None, None),
        P("lon", None, None),
    )
    out_specs = (P("lat", "lon", None), P("lat", "lon", None))
    return jax.shard_map(body, mesh=mesh, in_specs=in_specs, out_specs=out_specs, check_vma=False)
```

```python
import functools
import math

import jax
import jax.numpy as jnp
import numpy as np
from jax import lax
from jax.experimental import pallas as pl
from jax.experimental.pallas import tpu as pltpu
from jax.sharding import PartitionSpec as P

MESH = pl.DeviceIdType.MESH
F32 = jnp.float32
BF16 = jnp.bfloat16

DEG = 640
NLON = 1280
LAT = 64
LON = 16
ROWS = 10
COLS = 80
LEV = 128
OWN = 8
LEAD = 8
WIDE = 96
HID = 512
PACK = 14


def latitude_rows():
    row = np.arange(LAT * 16) % 16
    j = np.arange(LAT * 16) // 16 * ROWS + np.where(row < ROWS, row, row - ROWS)
    n = np.arange(DEG)
    phase = (n[None, :] * (2 * j[:, None] + 1)) % (4 * DEG)
    table = np.cos(phase * (math.pi / (2.0 * DEG))) * math.sqrt(2.0 / DEG)
    return table.astype(np.float32).astype(jnp.bfloat16)


def circle(turns):
    y = turns * math.pi
    z = y * y
    s = 1.0
    for k in (11, 9, 7, 5, 3):
        s = 1.0 - z * s * (1.0 / (k * (k - 1)))
    s = s * y
    c = 1.0
    for k in (12, 10, 8, 6, 4, 2):
        c = 1.0 - z * c * (1.0 / (k * (k - 1)))
    return 1.0 - 2.0 * s * s, 2.0 * s * c


def fraction(product):
    turns = product * (1.0 / NLON)
    return turns - jnp.floor(turns + 0.5)


def silu(v):
    half = 0.5 * v
    return half + half * jnp.tanh(half)


REACH = 8
NEAR = 4 * REACH + 1
FAR = LAT - 1 - NEAR


def rank_at(t, p, least, down_most, up_most):
    z, k = p // 2, t // 4
    low = jnp.minimum(z, down_most)
    down = jnp.where(k < low - least + 1, low - k, least + k)
    first = jnp.where(z > 31 - up_most, jnp.maximum(32 - z, least), least)
    up = jnp.where(first + k <= up_most, first + k, up_most - k)
    chip = lax.rem(z + jnp.where(lax.rem(t // 2, 2) == 0, 32 - down, up), 32)
    return chip * 2 + lax.rem(t, 2)


def near_rank(t, p):
    other = rank_at(t, p, 1, REACH, REACH)
    return jnp.where(t == NEAR - 1, p + 1 - 2 * lax.rem(p, 2), other)


def far_rank(t, p):
    return rank_at(t, p, REACH + 1, 16, 15)


def kernel(
    wave_ref,
    strength_ref,
    sunlit_ref,
    owner_ref,
    spectral_hbm,
    table_hbm,
    courant_hbm,
    win_hbm,
    wmid_hbm,
    wout_hbm,
    advected_hbm,
    heating_hbm,
    spec,
    table,
    cour,
    w_in,
    w_mid,
    w_out,
    damp,
    pay,
    got,
    gotf,
    wide,
    wide_low,
    trig,
    mcol,
    slab,
    land,
    land_south,
    land_north,
    c_north,
    c_south,
    c_west,
    c_east,
    flow,
    q_zero,
    q_one,
    adv,
    state,
    out_slots,
    in_slots,
    back_slots,
    ret_slots,
    heat,
    pick,
    place,
    local_sem,
    send_sem,
    recv_sem,
    heard,
):
    p = lax.axis_index("lat")
    q = lax.axis_index("lon")
    north = lax.rem(p + 1, LAT)
    south = lax.rem(p + LAT - 1, LAT)
    east = lax.rem(q + 1, LON)
    west = lax.rem(q + LON - 1, LON)

    get_spec = pltpu.make_async_copy(spectral_hbm, spec, local_sem.at[0])
    get_table = pltpu.make_async_copy(table_hbm, table, local_sem.at[1])
    get_cour = pltpu.make_async_copy(courant_hbm, cour, local_sem.at[2])
    get_in = pltpu.make_async_copy(win_hbm, w_in, local_sem.at[3])
    get_mid = pltpu.make_async_copy(wmid_hbm, w_mid, local_sem.at[4])
    get_out = pltpu.make_async_copy(wout_hbm, w_out, local_sem.at[5])
    get_spec.start()
    get_table.start()

    barrier = pltpu.get_barrier_semaphore()

    def greet_lat(t, carry):
        pl.semaphore_signal(barrier, inc=1, device_id=(near_rank(t, p), q), device_id_type=MESH)
        return carry

    lax.fori_loop(0, NEAR, greet_lat, 0)

    def greet_lon(t, carry):
        other = lax.rem(q + t, LON)
        pl.semaphore_signal(barrier, inc=1, device_id=(p, other), device_id_type=MESH)
        return carry

    lax.fori_loop(1, LON, greet_lon, 0)

    get_cour.start()
    get_in.start()
    get_mid.start()
    get_out.start()

    degree = lax.broadcasted_iota(jnp.int32, (OWN, DEG), 1)
    level = lax.broadcasted_iota(jnp.int32, (OWN, DEG), 0)
    strength = jnp.zeros((OWN, DEG), F32)
    for l in range(OWN):
        strength = jnp.where(level == l, strength_ref[l], strength)
    relative = (degree * (degree + 1)).astype(F32) / float(DEG * (DEG + 1))
    factor = 1.0 / (1.0 + strength * relative * relative)
    get_spec.wait()
    for s in range(ROWS):
        wave = wave_ref[p * ROWS + s]
        real = jnp.where(degree >= wave, spec[s, 0].astype(F32) * factor, 0.0)
        imag = jnp.where(
            degree >= jnp.where(wave > 0, wave, DEG), spec[s, 1].astype(F32) * factor, 0.0
        )
        both = jnp.concatenate([real, imag], axis=0).astype(BF16)
        damp[pl.ds(s * 16, 16), :] = both
        if s >= 8:
            damp[pl.ds(s * 16 + 32, 16), :] = both
            damp[pl.ds(s * 16 + 64, 16), :] = both
    damp[pl.ds(224, 32), :] = jnp.zeros((32, DEG), BF16)

    get_table.wait()
    row16 = lax.broadcasted_iota(jnp.int32, (LAT * 16, LEV), 0) % 16
    lane = lax.broadcasted_iota(jnp.int32, (LAT * 16, LEV), 1)
    y = lax.dot_general(
        table[...], damp[...], (((1,), (1,)), ((), ())), preferred_element_type=F32
    )
    first, last = y[:, :128], y[:, 128:]
    tail = jnp.where(
        lane < 32, last, jnp.where(lane < 64, pltpu.roll(last, 6, 0), pltpu.roll(last, 2, 0))
    )
    packed = jnp.where(row16 < ROWS, first, tail).astype(BF16)
    pay[...] = packed.reshape(LAT, 8, 2, LEV)[:, : PACK // 2]

    get_cour.wait()
    pl.semaphore_wait(barrier, NEAR + LON - 1)
    for d in (REACH, 32 - REACH):
        pl.semaphore_signal(
            heard, inc=1, device_id=(lax.rem(p + 2 * d, LAT), q), device_id_type=MESH
        )

    edge_north = pltpu.make_async_remote_copy(
        cour.at[:, ROWS - 1],
        c_south,
        send_sem.at[1],
        recv_sem.at[1],
        device_id=(north, q),
        device_id_type=MESH,
    )
    edge_south = pltpu.make_async_remote_copy(
        cour.at[:, 0],
        c_north,
        send_sem.at[2],
        recv_sem.at[2],
        device_id=(south, q),
        device_id_type=MESH,
    )
    edge_east = pltpu.make_async_remote_copy(
        cour.at[:, :, pl.ds(COLS - 16, 16), :],
        c_west,
        send_sem.at[3],
        recv_sem.at[3],
        device_id=(p, east),
        device_id_type=MESH,
    )
    edge_west = pltpu.make_async_remote_copy(
        cour.at[:, :, pl.ds(0, 16), :],
        c_east,
        send_sem.at[4],
        recv_sem.at[4],
        device_id=(p, west),
        device_id_type=MESH,
    )
    def send_lat(rank_of, t, carry):
        other = rank_of(t, p)
        pltpu.make_async_remote_copy(
            pay.at[other],
            got.at[p],
            send_sem.at[0],
            recv_sem.at[0],
            device_id=(other, q),
            device_id_type=MESH,
        ).start()
        return carry

    lax.fori_loop(0, NEAR, functools.partial(send_lat, near_rank), 0)
    pltpu.make_async_copy(pay.at[p], got.at[p], recv_sem.at[0]).start()

    edge_east.start()
    edge_west.start()

    sub8 = lax.broadcasted_iota(jnp.int32, (8, LEV), 0)

    def columns(t, carry):
        s, group = t // 8, lax.rem(t, 8)
        value = jnp.zeros((8, LEV), jnp.int32)
        for r in range(8):
            value = jnp.where(sub8 == r, wave_ref[(group * 8 + r) * ROWS + s], value)
        mcol[pl.ds(pl.multiple_of(t * 8, 8), 8), :] = value.astype(F32)
        return carry

    lax.fori_loop(0, 80, columns, 0)

    shift = (lax.broadcasted_iota(jnp.int32, (64, LEV), 1) - LEAD).astype(F32)
    scale = 1.0 / math.sqrt(DEG)

    def trig_rows(s, carry):
        m = mcol[pl.ds(pl.multiple_of(s * 64, 64), 64), :]
        c, d = circle(fraction(m * shift))
        c, d = c * scale, d * scale
        c1, d1 = circle(fraction(m * float(COLS)))
        base = pl.multiple_of(s * 128, 128)
        for other in range(LON):
            lanes = pl.ds((other % 4) * 128, 128)
            trig[other // 4, pl.ds(base, 64), lanes] = c.astype(BF16)
            trig[other // 4, pl.ds(base + 64, 64), lanes] = (-d).astype(BF16)
            c, d = c * c1 - d * d1, d * c1 + c * d1
        return carry

    lax.fori_loop(0, ROWS, trig_rows, 0)

    pl.semaphore_wait(heard, 2)
    lax.fori_loop(0, FAR, functools.partial(send_lat, far_rank), 0)
    @pl.when(p < LAT - 1)
    def _():
        edge_north.start()

    @pl.when(p > 0)
    def _():
        edge_south.start()

    owners = [owner_ref[t] for t in range(12)]
    listed = [sunlit_ref[t] for t in range(12)]
    slots = []
    for t in range(12):
        rank = jnp.int32(0)
        for u in range(t):
            rank = rank + (owners[u] == owners[t]).astype(jnp.int32)
        slots.append(owners[t] * 2 + rank)

    def fill_pick(k, carry):
        value = jnp.int32(0)
        for t in range(12):
            value = jnp.where(slots[t] == k, listed[t], value)
        pick[k] = value
        return carry

    lax.fori_loop(0, 32, fill_pick, 0)

    def fill_place(k, carry):
        value = jnp.int32(32)
        for t in range(12):
            value = jnp.where(listed[t] == k, slots[t], value)
        place[k] = value
        return carry

    lax.fori_loop(0, 50, fill_place, 0)

    edge_east.wait()
    edge_west.wait()
    zeros8 = jnp.zeros((8, LEV), F32)

    def edge_row(at, edge):
        for k in range(2):
            flow[k, at] = jnp.concatenate([zeros8, edge[k].astype(F32), zeros8], axis=0)

    def fill_flow(r, carry):
        for k in range(2):
            flow[k, r + 1] = jnp.concatenate(
                [
                    c_west[k, r].astype(F32)[8:],
                    cour[k, r].astype(F32),
                    c_east[k, r].astype(F32)[:8],
                ],
                axis=0,
            )
        return carry

    lax.fori_loop(0, ROWS, fill_flow, 0)

    pltpu.make_async_copy(got, got, recv_sem.at[0]).wait()
    gotf[...] = got[...].astype(F32).reshape(LAT * PACK, LEV)
    low = lax.broadcasted_iota(jnp.int32, (8, LEV), 1) < 64
    for r in range(PACK):
        part = gotf[pl.ds(r, LAT, stride=PACK), :]
        turned = jnp.concatenate([part, part], axis=0).T
        if r < ROWS:
            for a in range(8):
                wide[pl.ds(r * 8, 8), pl.ds(a * 128, 128)] = jnp.where(
                    low, turned[a * 16 : a * 16 + 8], turned[a * 16 + 8 : a * 16 + 16]
                )
        else:
            for g, jj in enumerate(range(r - ROWS, ROWS, 4)):
                for a in range(2):
                    at = g * 32 + a * 16
                    wide[pl.ds(jj * 8, 8), pl.ds((8 + a) * 128, 128)] = jnp.where(
                        low, turned[at : at + 8], turned[at + 8 : at + 16]
                    )

    wide_low[...] = wide[...].astype(BF16)

    def send_lon(t, carry):
        four = lax.rem(q // 4 + t, LON // 4)
        g = jnp.dot(wide_low[...], trig[four], preferred_element_type=F32).astype(BF16)
        for h in range(4):
            other = four * 4 + h
            slab[other] = g[:, h * 128 : (h + 1) * 128]

            @pl.when(other != q)
            def _():
                pltpu.make_async_remote_copy(
                    slab.at[other],
                    land.at[q],
                    send_sem.at[5],
                    recv_sem.at[5],
                    device_id=(p, other),
                    device_id_type=MESH,
                ).start()

            @pl.when(other == q)
            def _():
                pltpu.make_async_copy(
                    slab.at[other], land.at[q], recv_sem.at[5]
                ).start()

            @pl.when(p < LAT - 1)
            def _():
                pltpu.make_async_remote_copy(
                    slab.at[other, pl.ds(64, 16), :],
                    land_south.at[q],
                    send_sem.at[8],
                    recv_sem.at[8],
                    device_id=(north, other),
                    device_id_type=MESH,
                ).start()

            @pl.when(p > 0)
            def _():
                pltpu.make_async_remote_copy(
                    slab.at[other, pl.ds(0, 16), :],
                    land_north.at[q],
                    send_sem.at[9],
                    recv_sem.at[9],
                    device_id=(south, other),
                    device_id_type=MESH,
                ).start()

        return carry

    lax.fori_loop(0, LON // 4, send_lon, 0)
    def assemble(two, at):
        for k in range(2):
            q_zero[at + k] = two[:, k * 8 : k * 8 + 8, :].reshape(128, 128).T[:WIDE]

    pltpu.make_async_copy(land, land, recv_sem.at[5]).wait()
    for h in range(5):
        assemble(land[:, pl.ds(h * 16, 16), :].astype(F32), 2 + h * 2)

    @pl.when(p > 0)
    def _():
        pltpu.make_async_copy(land_south, land_south, recv_sem.at[8]).wait()
        assemble(land_south[...].astype(F32), 0)
        edge_south.wait_send()
        edge_north.wait_recv()
        edge_row(0, c_south)

    @pl.when(p == 0)
    def _():
        q_zero[pl.ds(0, 2)] = jnp.zeros((2, WIDE, LEV), F32)
        flow[0, 0] = jnp.zeros((WIDE, LEV), F32)
        flow[1, 0] = jnp.zeros((WIDE, LEV), F32)

    @pl.when(p < LAT - 1)
    def _():
        pltpu.make_async_copy(land_north, land_north, recv_sem.at[9]).wait()
        assemble(land_north[...].astype(F32), ROWS + 2)
        edge_north.wait_send()
        edge_south.wait_recv()
        edge_row(ROWS + 1, c_north)

    @pl.when(p == LAT - 1)
    def _():
        q_zero[pl.ds(ROWS + 2, 2)] = jnp.zeros((2, WIDE, LEV), F32)
        flow[0, ROWS + 1] = jnp.zeros((WIDE, LEV), F32)
        flow[1, ROWS + 1] = jnp.zeros((WIDE, LEV), F32)

    def step(centre, upper, lower, u, v):
        right = pltpu.roll(centre, WIDE - 1, 0)
        left = pltpu.roll(centre, 1, 0)
        along = centre - 0.5 * u * (right - left) + 0.5 * u * u * (right - 2.0 * centre + left)
        return (
            along - 0.5 * v * (upper - lower) + 0.5 * v * v * (upper - 2.0 * centre + lower)
        )

    def first_step(r, carry):
        q_one[r] = step(q_zero[r + 1], q_zero[r + 2], q_zero[r], flow[0, r], flow[1, r])
        return carry

    lax.fori_loop(0, ROWS + 2, first_step, 0)
    q_one[0] = jnp.where(p == 0, 0.0, q_one[0])
    q_one[ROWS + 1] = jnp.where(p == LAT - 1, 0.0, q_one[ROWS + 1])

    def second_step(r, carry):
        new = step(q_one[r + 1], q_one[r + 2], q_one[r], flow[0, r + 1], flow[1, r + 1])
        new = new[LEAD : LEAD + COLS]
        adv[r] = new
        state[pl.ds(r * 5, 5)] = new.astype(BF16).reshape(5, 16, LEV)
        return carry

    lax.fori_loop(0, ROWS, second_step, 0)
    put_adv = pltpu.make_async_copy(adv, advected_hbm, local_sem.at[6])
    put_adv.start()

    def pack(other):
        for k in range(2):
            out_slots[other * 2 + k] = state[pick[other * 2 + k]]

    def send_out(t, carry):
        other = lax.rem(q + t, LON)
        pack(other)
        pltpu.make_async_remote_copy(
            out_slots.at[pl.ds(other * 2, 2)],
            in_slots.at[pl.ds(q * 2, 2)],
            send_sem.at[6],
            recv_sem.at[6],
            device_id=(p, other),
            device_id_type=MESH,
        ).start()
        return carry

    lax.fori_loop(1, LON, send_out, 0)
    pack(q)
    pltpu.make_async_copy(
        out_slots.at[pl.ds(q * 2, 2)], in_slots.at[pl.ds(q * 2, 2)], recv_sem.at[6]
    ).start()
    get_in.wait()
    get_mid.wait()
    get_out.wait()
    pltpu.make_async_copy(in_slots, in_slots, recv_sem.at[6]).wait()
    x = in_slots[...].reshape(HID, LEV)
    one = silu(jnp.dot(x, w_in[0], preferred_element_type=F32)).astype(BF16)
    two = silu(jnp.dot(one, w_mid[0], preferred_element_type=F32)).astype(BF16)
    three = jnp.dot(two, w_out[0], preferred_element_type=F32).astype(BF16)
    back_slots[...] = three.reshape(2 * LON, 16, LEV)

    def send_back(t, carry):
        other = lax.rem(q + t, LON)
        pltpu.make_async_remote_copy(
            back_slots.at[pl.ds(other * 2, 2)],
            ret_slots.at[pl.ds(q * 2, 2)],
            send_sem.at[7],
            recv_sem.at[7],
            device_id=(p, other),
            device_id_type=MESH,
        ).start()
        return carry

    lax.fori_loop(1, LON, send_back, 0)
    pltpu.make_async_copy(
        back_slots.at[pl.ds(q * 2, 2)], ret_slots.at[pl.ds(q * 2, 2)], recv_sem.at[7]
    ).start()
    ret_slots[2 * LON] = jnp.zeros((16, LEV), BF16)
    some = pl.ds(0, 2 * LON)
    pltpu.make_async_copy(ret_slots.at[some], ret_slots.at[some], recv_sem.at[7]).wait()

    def unpack(r, carry):
        for k in range(5):
            heat[r, pl.ds(k * 16, 16), :] = ret_slots[place[r * 5 + k]]
        return carry

    lax.fori_loop(0, ROWS, unpack, 0)
    put_heat = pltpu.make_async_copy(heat, heating_hbm, local_sem.at[7])
    put_heat.start()

    sent = pl.ds(0, LAT - 1)
    pltpu.make_async_copy(pay.at[sent], pay.at[sent], send_sem.at[0]).wait()
    sent = pl.ds(0, LON - 1)
    pltpu.make_async_copy(slab.at[sent], slab.at[sent], send_sem.at[5]).wait()

    @pl.when(p < LAT - 1)
    def _():
        pltpu.make_async_copy(land_south, land_south, send_sem.at[8]).wait()

    @pl.when(p > 0)
    def _():
        pltpu.make_async_copy(land_north, land_north, send_sem.at[9]).wait()

    sent = pl.ds(0, 2 * LON - 2)
    pltpu.make_async_copy(out_slots.at[sent], out_slots.at[sent], send_sem.at[6]).wait()
    pltpu.make_async_copy(back_slots.at[sent], back_slots.at[sent], send_sem.at[7]).wait()
    put_adv.wait()
    put_heat.wait()


def hand_out(advected_hbm, heating_hbm, advected_out, heating_out, adv, heat, in_sem, out_sem):
    ways = []
    for k in range(2):
        part = pl.ds(k * (ROWS // 2), ROWS // 2)
        for source, held, target, at in (
            (advected_hbm, adv, advected_out, k),
            (heating_hbm, heat, heating_out, 2 + k),
        ):
            ways.append(
                (
                    pltpu.make_async_copy(source.at[part], held.at[part], in_sem.at[at]),
                    pltpu.make_async_copy(held.at[part], target.at[part], out_sem.at[at]),
                )
            )
    for there, _ in ways:
        there.start()
    for there, back in ways:
        there.wait()
        back.start()
    for _, back in ways:
        back.wait()


def body(
    spectral,
    wavenumber_of_slot,
    filter_strength,
    courant,
    sunlit_blocks,
    sunlit_owner,
    radiation_in,
    radiation_mid,
    radiation_out,
):
    smem = pl.BlockSpec(memory_space=pltpu.SMEM)
    anywhere = pl.BlockSpec(memory_space=pl.ANY)
    dma = pltpu.SemaphoreType.DMA
    outs = (
        jax.ShapeDtypeStruct((ROWS, COLS, LEV), F32),
        jax.ShapeDtypeStruct((ROWS, COLS, LEV), BF16),
    )
    advected, heating = pl.pallas_call(
        kernel,
        out_shape=outs,
        in_specs=[smem] * 4 + [anywhere] * 6,
        out_specs=(anywhere, anywhere),
        scratch_shapes=[
            pltpu.VMEM((ROWS, 2, OWN, DEG), BF16),
            pltpu.VMEM((LAT * 16, DEG), BF16),
            pltpu.VMEM((2, ROWS, COLS, LEV), BF16),
            pltpu.VMEM((1, LEV, HID), BF16),
            pltpu.VMEM((1, HID, HID), BF16),
            pltpu.VMEM((1, HID, LEV), BF16),
            pltpu.VMEM((256, DEG), BF16),
            pltpu.VMEM((LAT, PACK // 2, 2, LEV), BF16),
            pltpu.VMEM((LAT, PACK // 2, 2, LEV), BF16),
            pltpu.VMEM((LAT * PACK, LEV), F32),
            pltpu.VMEM((COLS, NLON), F32),
            pltpu.VMEM((COLS, NLON), BF16),
            pltpu.VMEM((LON // 4, NLON, 512), BF16),
            pltpu.VMEM((DEG, LEV), F32),
            pltpu.VMEM((LON, COLS, LEV), BF16),
            pltpu.VMEM((LON, COLS, LEV), BF16),
            pltpu.VMEM((LON, 16, LEV), BF16),
            pltpu.VMEM((LON, 16, LEV), BF16),
            pltpu.VMEM((2, COLS, LEV), BF16),
            pltpu.VMEM((2, COLS, LEV), BF16),
            pltpu.VMEM((2, ROWS, 16, LEV), BF16),
            pltpu.VMEM((2, ROWS, 16, LEV), BF16),
            pltpu.VMEM((2, ROWS + 2, WIDE, LEV), F32),
            pltpu.VMEM((ROWS + 4, WIDE, LEV), F32),
            pltpu.VMEM((ROWS + 2, WIDE, LEV), F32),
            pltpu.VMEM((ROWS, COLS, LEV), F32),
            pltpu.VMEM((50, 16, LEV), BF16),
            pltpu.VMEM((2 * LON, 16, LEV), BF16),
            pltpu.VMEM((2 * LON, 16, LEV), BF16),
            pltpu.VMEM((2 * LON, 16, LEV), BF16),
            pltpu.VMEM((2 * LON + 1, 16, LEV), BF16),
            pltpu.VMEM((ROWS, COLS, LEV), BF16),
            pltpu.SMEM((32,), jnp.int32),
            pltpu.SMEM((50,), jnp.int32),
            dma((8,)),
            dma((10,)),
            dma((10,)),
            pltpu.SemaphoreType.REGULAR,
        ],
        compiler_params=pltpu.CompilerParams(
            collective_id=1, has_side_effects=True, vmem_limit_bytes=64 * 1024 * 1024
        ),
        name="spectral_radiation",
    )(
        wavenumber_of_slot,
        filter_strength,
        sunlit_blocks.reshape(-1),
        sunlit_owner.reshape(-1),
        spectral,
        jnp.asarray(latitude_rows()),
        courant,
        radiation_in,
        radiation_mid,
        radiation_out,
    )
    return pl.pallas_call(
        hand_out,
        out_shape=outs,
        in_specs=[anywhere] * 2,
        out_specs=(anywhere, anywhere),
        scratch_shapes=[
            pltpu.VMEM((ROWS, COLS, LEV), F32),
            pltpu.VMEM((ROWS, COLS, LEV), BF16),
            dma((4,)),
            dma((4,)),
        ],
        name="hand_out",
        compiler_params=pltpu.CompilerParams(vmem_limit_bytes=64 * 1024 * 1024),
    )(advected, heating)


def solution(mesh):
    in_specs = (
        P("lat", None, "lon", None),
        P(),
        P("lon"),
        P(None, "lat", "lon", None),
        P("lat", "lon", None),
        P("lat", "lon", None, None),
        P("lon", None, None),
        P("lon", None, None),
        P("lon", None, None),
    )
    out_specs = (P("lat", "lon", None), P("lat", "lon", None))
    return jax.shard_map(body, mesh=mesh, in_specs=in_specs, out_specs=out_specs, check_vma=False)
```

```python
import functools
import math

import jax
import jax.numpy as jnp
import numpy as np
from jax import lax
from jax.experimental import pallas as pl
from jax.experimental.pallas import tpu as pltpu
from jax.sharding import PartitionSpec as P

MESH = pl.DeviceIdType.MESH
F32 = jnp.float32
BF16 = jnp.bfloat16

DEG = 640
NLON = 1280
LAT = 64
LON = 16
ROWS = 10
COLS = 80
LEV = 128
OWN = 8
LEAD = 8
WIDE = 96
HID = 512
PACK = 14


def latitude_rows():
    row = np.arange(LAT * 16) % 16
    j = np.arange(LAT * 16) // 16 * ROWS + np.where(row < ROWS, row, row - ROWS)
    n = np.arange(DEG)
    phase = (n[None, :] * (2 * j[:, None] + 1)) % (4 * DEG)
    table = np.cos(phase * (math.pi / (2.0 * DEG))) * math.sqrt(2.0 / DEG)
    return table.astype(np.float32).astype(jnp.bfloat16)


def circle(turns):
    y = turns * math.pi
    z = y * y
    s = 1.0
    for k in (11, 9, 7, 5, 3):
        s = 1.0 - z * s * (1.0 / (k * (k - 1)))
    s = s * y
    c = 1.0
    for k in (12, 10, 8, 6, 4, 2):
        c = 1.0 - z * c * (1.0 / (k * (k - 1)))
    return 1.0 - 2.0 * s * s, 2.0 * s * c


def fraction(product):
    turns = product * (1.0 / NLON)
    return turns - jnp.floor(turns + 0.5)


def silu(v):
    half = 0.5 * v
    return half + half * jnp.tanh(half)


REACH = 8
NEAR = 4 * REACH + 1
FAR = LAT - 1 - NEAR


def rank_at(t, p, least, down_most, up_most):
    z, k = p // 2, t // 4
    low = jnp.minimum(z, down_most)
    down = jnp.where(k < low - least + 1, low - k, least + k)
    first = jnp.where(z > 31 - up_most, jnp.maximum(32 - z, least), least)
    up = jnp.where(first + k <= up_most, first + k, up_most - k)
    chip = lax.rem(z + jnp.where(lax.rem(t // 2, 2) == 0, 32 - down, up), 32)
    return chip * 2 + lax.rem(t, 2)


def near_rank(t, p):
    other = rank_at(t, p, 1, REACH, REACH)
    return jnp.where(t == NEAR - 1, p + 1 - 2 * lax.rem(p, 2), other)


def far_rank(t, p):
    return rank_at(t, p, REACH + 1, 16, 15)


def kernel(
    wave_ref,
    strength_ref,
    sunlit_ref,
    owner_ref,
    spectral_hbm,
    table_hbm,
    courant_hbm,
    win_hbm,
    wmid_hbm,
    wout_hbm,
    advected_hbm,
    heating_hbm,
    spec,
    table,
    cour,
    w_in,
    w_mid,
    w_out,
    damp,
    pay,
    got,
    gotf,
    wide,
    wide_low,
    trig,
    mcol,
    slab,
    land,
    land_south,
    land_north,
    c_north,
    c_south,
    c_west,
    c_east,
    flow,
    q_zero,
    q_one,
    adv,
    state,
    out_slots,
    in_slots,
    back_slots,
    ret_slots,
    heat,
    pick,
    place,
    local_sem,
    send_sem,
    recv_sem,
    heard,
):
    p = lax.axis_index("lat")
    q = lax.axis_index("lon")
    north = lax.rem(p + 1, LAT)
    south = lax.rem(p + LAT - 1, LAT)
    east = lax.rem(q + 1, LON)
    west = lax.rem(q + LON - 1, LON)

    get_spec = pltpu.make_async_copy(spectral_hbm, spec, local_sem.at[0])
    get_table = pltpu.make_async_copy(table_hbm, table, local_sem.at[1])
    get_cour = pltpu.make_async_copy(courant_hbm, cour, local_sem.at[2])
    get_in = pltpu.make_async_copy(win_hbm, w_in, local_sem.at[3])
    get_mid = pltpu.make_async_copy(wmid_hbm, w_mid, local_sem.at[4])
    get_out = pltpu.make_async_copy(wout_hbm, w_out, local_sem.at[5])
    get_spec.start()
    get_table.start()

    barrier = pltpu.get_barrier_semaphore()

    def greet_lat(t, carry):
        pl.semaphore_signal(barrier, inc=1, device_id=(near_rank(t, p), q), device_id_type=MESH)
        return carry

    lax.fori_loop(0, NEAR, greet_lat, 0)

    def greet_lon(t, carry):
        other = lax.rem(q + t, LON)
        pl.semaphore_signal(barrier, inc=1, device_id=(p, other), device_id_type=MESH)
        return carry

    lax.fori_loop(1, LON, greet_lon, 0)

    get_cour.start()
    get_in.start()
    get_mid.start()
    get_out.start()

    degree = lax.broadcasted_iota(jnp.int32, (OWN, DEG), 1)
    level = lax.broadcasted_iota(jnp.int32, (OWN, DEG), 0)
    strength = jnp.zeros((OWN, DEG), F32)
    for l in range(OWN):
        strength = jnp.where(level == l, strength_ref[l], strength)
    relative = (degree * (degree + 1)).astype(F32) / float(DEG * (DEG + 1))
    factor = 1.0 / (1.0 + strength * relative * relative)
    get_spec.wait()
    for s in range(ROWS):
        wave = wave_ref[p * ROWS + s]
        real = jnp.where(degree >= wave, spec[s, 0].astype(F32) * factor, 0.0)
        imag = jnp.where(
            degree >= jnp.where(wave > 0, wave, DEG), spec[s, 1].astype(F32) * factor, 0.0
        )
        both = jnp.concatenate([real, imag], axis=0).astype(BF16)
        damp[pl.ds(s * 16, 16), :] = both
        if s >= 8:
            damp[pl.ds(s * 16 + 32, 16), :] = both
            damp[pl.ds(s * 16 + 64, 16), :] = both
    damp[pl.ds(224, 32), :] = jnp.zeros((32, DEG), BF16)

    get_table.wait()
    row16 = lax.broadcasted_iota(jnp.int32, (LAT * 16, LEV), 0) % 16
    lane = lax.broadcasted_iota(jnp.int32, (LAT * 16, LEV), 1)
    y = lax.dot_general(
        table[...], damp[...], (((1,), (1,)), ((), ())), preferred_element_type=F32
    )
    first, last = y[:, :128], y[:, 128:]
    tail = jnp.where(
        lane < 32, last, jnp.where(lane < 64, pltpu.roll(last, 6, 0), pltpu.roll(last, 2, 0))
    )
    packed = jnp.where(row16 < ROWS, first, tail).astype(BF16)
    pay[...] = packed.reshape(LAT, 8, 2, LEV)[:, : PACK // 2]

    get_cour.wait()
    pl.semaphore_wait(barrier, NEAR + LON - 1)
    for d in (REACH, 32 - REACH):
        pl.semaphore_signal(
            heard, inc=1, device_id=(lax.rem(p + 2 * d, LAT), q), device_id_type=MESH
        )

    edge_north = pltpu.make_async_remote_copy(
        cour.at[:, ROWS - 1],
        c_south,
        send_sem.at[1],
        recv_sem.at[1],
        device_id=(north, q),
        device_id_type=MESH,
    )
    edge_south = pltpu.make_async_remote_copy(
        cour.at[:, 0],
        c_north,
        send_sem.at[2],
        recv_sem.at[2],
        device_id=(south, q),
        device_id_type=MESH,
    )
    edge_east = pltpu.make_async_remote_copy(
        cour.at[:, :, pl.ds(COLS - 16, 16), :],
        c_west,
        send_sem.at[3],
        recv_sem.at[3],
        device_id=(p, east),
        device_id_type=MESH,
    )
    edge_west = pltpu.make_async_remote_copy(
        cour.at[:, :, pl.ds(0, 16), :],
        c_east,
        send_sem.at[4],
        recv_sem.at[4],
        device_id=(p, west),
        device_id_type=MESH,
    )
    def send_lat(rank_of, t, carry):
        other = rank_of(t, p)
        pltpu.make_async_remote_copy(
            pay.at[other],
            got.at[p],
            send_sem.at[0],
            recv_sem.at[0],
            device_id=(other, q),
            device_id_type=MESH,
        ).start()
        return carry

    lax.fori_loop(0, NEAR, functools.partial(send_lat, near_rank), 0)
    pltpu.make_async_copy(pay.at[p], got.at[p], recv_sem.at[0]).start()

    edge_east.start()
    edge_west.start()

    pl.semaphore_wait(heard, 2)
    lax.fori_loop(0, FAR, functools.partial(send_lat, far_rank), 0)
    @pl.when(p < LAT - 1)
    def _():
        edge_north.start()

    @pl.when(p > 0)
    def _():
        edge_south.start()

    sub8 = lax.broadcasted_iota(jnp.int32, (8, LEV), 0)

    def columns(t, carry):
        s, group = t // 8, lax.rem(t, 8)
        value = jnp.zeros((8, LEV), jnp.int32)
        for r in range(8):
            value = jnp.where(sub8 == r, wave_ref[(group * 8 + r) * ROWS + s], value)
        mcol[pl.ds(pl.multiple_of(t * 8, 8), 8), :] = value.astype(F32)
        return carry

    lax.fori_loop(0, 80, columns, 0)

    shift = (lax.broadcasted_iota(jnp.int32, (64, LEV), 1) - LEAD).astype(F32)
    scale = 1.0 / math.sqrt(DEG)

    def trig_rows(s, carry):
        m = mcol[pl.ds(pl.multiple_of(s * 64, 64), 64), :]
        c, d = circle(fraction(m * shift))
        c, d = c * scale, d * scale
        c1, d1 = circle(fraction(m * float(COLS)))
        base = pl.multiple_of(s * 128, 128)
        for other in range(LON):
            lanes = pl.ds((other % 4) * 128, 128)
            trig[other // 4, pl.ds(base, 64), lanes] = c.astype(BF16)
            trig[other // 4, pl.ds(base + 64, 64), lanes] = (-d).astype(BF16)
            c, d = c * c1 - d * d1, d * c1 + c * d1
        return carry

    lax.fori_loop(0, ROWS, trig_rows, 0)

    owners = [owner_ref[t] for t in range(12)]
    listed = [sunlit_ref[t] for t in range(12)]
    slots = []
    for t in range(12):
        rank = jnp.int32(0)
        for u in range(t):
            rank = rank + (owners[u] == owners[t]).astype(jnp.int32)
        slots.append(owners[t] * 2 + rank)

    def fill_pick(k, carry):
        value = jnp.int32(0)
        for t in range(12):
            value = jnp.where(slots[t] == k, listed[t], value)
        pick[k] = value
        return carry

    lax.fori_loop(0, 32, fill_pick, 0)

    def fill_place(k, carry):
        value = jnp.int32(32)
        for t in range(12):
            value = jnp.where(listed[t] == k, slots[t], value)
        place[k] = value
        return carry

    lax.fori_loop(0, 50, fill_place, 0)

    edge_east.wait()
    edge_west.wait()
    zeros8 = jnp.zeros((8, LEV), F32)

    def edge_row(at, edge):
        for k in range(2):
            flow[k, at] = jnp.concatenate([zeros8, edge[k].astype(F32), zeros8], axis=0)

    def fill_flow(r, carry):
        for k in range(2):
            flow[k, r + 1] = jnp.concatenate(
                [
                    c_west[k, r].astype(F32)[8:],
                    cour[k, r].astype(F32),
                    c_east[k, r].astype(F32)[:8],
                ],
                axis=0,
            )
        return carry

    lax.fori_loop(0, ROWS, fill_flow, 0)

    pltpu.make_async_copy(got, got, recv_sem.at[0]).wait()
    gotf[...] = got[...].astype(F32).reshape(LAT * PACK, LEV)
    low = lax.broadcasted_iota(jnp.int32, (8, LEV), 1) < 64
    for r in range(PACK):
        part = gotf[pl.ds(r, LAT, stride=PACK), :]
        turned = jnp.concatenate([part, part], axis=0).T
        if r < ROWS:
            for a in range(8):
                wide[pl.ds(r * 8, 8), pl.ds(a * 128, 128)] = jnp.where(
                    low, turned[a * 16 : a * 16 + 8], turned[a * 16 + 8 : a * 16 + 16]
                )
        else:
            for g, jj in enumerate(range(r - ROWS, ROWS, 4)):
                for a in range(2):
                    at = g * 32 + a * 16
                    wide[pl.ds(jj * 8, 8), pl.ds((8 + a) * 128, 128)] = jnp.where(
                        low, turned[at : at + 8], turned[at + 8 : at + 16]
                    )

    wide_low[...] = wide[...].astype(BF16)

    def send_lon(t, carry):
        four = lax.rem(q // 4 + t, LON // 4)
        g = jnp.dot(wide_low[...], trig[four], preferred_element_type=F32).astype(BF16)
        for h in range(4):
            other = four * 4 + h
            slab[other] = g[:, h * 128 : (h + 1) * 128]

            @pl.when(other != q)
            def _():
                pltpu.make_async_remote_copy(
                    slab.at[other],
                    land.at[q],
                    send_sem.at[5],
                    recv_sem.at[5],
                    device_id=(p, other),
                    device_id_type=MESH,
                ).start()

            @pl.when(other == q)
            def _():
                pltpu.make_async_copy(
                    slab.at[other], land.at[q], recv_sem.at[5]
                ).start()

            @pl.when(p < LAT - 1)
            def _():
                pltpu.make_async_remote_copy(
                    slab.at[other, pl.ds(64, 16), :],
                    land_south.at[q],
                    send_sem.at[8],
                    recv_sem.at[8],
                    device_id=(north, other),
                    device_id_type=MESH,
                ).start()

            @pl.when(p > 0)
            def _():
                pltpu.make_async_remote_copy(
                    slab.at[other, pl.ds(0, 16), :],
                    land_north.at[q],
                    send_sem.at[9],
                    recv_sem.at[9],
                    device_id=(south, other),
                    device_id_type=MESH,
                ).start()

        return carry

    lax.fori_loop(0, LON // 4, send_lon, 0)
    def assemble(two, at):
        for k in range(2):
            q_zero[at + k] = two[:, k * 8 : k * 8 + 8, :].reshape(128, 128).T[:WIDE]

    pltpu.make_async_copy(land, land, recv_sem.at[5]).wait()
    for h in range(5):
        assemble(land[:, pl.ds(h * 16, 16), :].astype(F32), 2 + h * 2)

    @pl.when(p > 0)
    def _():
        pltpu.make_async_copy(land_south, land_south, recv_sem.at[8]).wait()
        assemble(land_south[...].astype(F32), 0)
        edge_south.wait_send()
        edge_north.wait_recv()
        edge_row(0, c_south)

    @pl.when(p == 0)
    def _():
        q_zero[pl.ds(0, 2)] = jnp.zeros((2, WIDE, LEV), F32)
        flow[0, 0] = jnp.zeros((WIDE, LEV), F32)
        flow[1, 0] = jnp.zeros((WIDE, LEV), F32)

    @pl.when(p < LAT - 1)
    def _():
        pltpu.make_async_copy(land_north, land_north, recv_sem.at[9]).wait()
        assemble(land_north[...].astype(F32), ROWS + 2)
        edge_north.wait_send()
        edge_south.wait_recv()
        edge_row(ROWS + 1, c_north)

    @pl.when(p == LAT - 1)
    def _():
        q_zero[pl.ds(ROWS + 2, 2)] = jnp.zeros((2, WIDE, LEV), F32)
        flow[0, ROWS + 1] = jnp.zeros((WIDE, LEV), F32)
        flow[1, ROWS + 1] = jnp.zeros((WIDE, LEV), F32)

    def step(centre, upper, lower, u, v):
        right = pltpu.roll(centre, WIDE - 1, 0)
        left = pltpu.roll(centre, 1, 0)
        along = centre - 0.5 * u * (right - left) + 0.5 * u * u * (right - 2.0 * centre + left)
        return (
            along - 0.5 * v * (upper - lower) + 0.5 * v * v * (upper - 2.0 * centre + lower)
        )

    def first_step(r, carry):
        q_one[r] = step(q_zero[r + 1], q_zero[r + 2], q_zero[r], flow[0, r], flow[1, r])
        return carry

    lax.fori_loop(0, ROWS + 2, first_step, 0)
    q_one[0] = jnp.where(p == 0, 0.0, q_one[0])
    q_one[ROWS + 1] = jnp.where(p == LAT - 1, 0.0, q_one[ROWS + 1])

    def second_step(r, carry):
        new = step(q_one[r + 1], q_one[r + 2], q_one[r], flow[0, r + 1], flow[1, r + 1])
        new = new[LEAD : LEAD + COLS]
        adv[r] = new
        state[pl.ds(r * 5, 5)] = new.astype(BF16).reshape(5, 16, LEV)
        return carry

    lax.fori_loop(0, ROWS, second_step, 0)
    put_adv = pltpu.make_async_copy(adv, advected_hbm, local_sem.at[6])
    put_adv.start()

    def pack(other):
        for k in range(2):
            out_slots[other * 2 + k] = state[pick[other * 2 + k]]

    def send_out(t, carry):
        other = lax.rem(q + t, LON)
        pack(other)
        pltpu.make_async_remote_copy(
            out_slots.at[pl.ds(other * 2, 2)],
            in_slots.at[pl.ds(q * 2, 2)],
            send_sem.at[6],
            recv_sem.at[6],
            device_id=(p, other),
            device_id_type=MESH,
        ).start()
        return carry

    lax.fori_loop(1, LON, send_out, 0)
    pack(q)
    pltpu.make_async_copy(
        out_slots.at[pl.ds(q * 2, 2)], in_slots.at[pl.ds(q * 2, 2)], recv_sem.at[6]
    ).start()
    get_in.wait()
    get_mid.wait()
    get_out.wait()
    pltpu.make_async_copy(in_slots, in_slots, recv_sem.at[6]).wait()
    x = in_slots[...].reshape(HID, LEV)
    one = silu(jnp.dot(x, w_in[0], preferred_element_type=F32)).astype(BF16)
    two = silu(jnp.dot(one, w_mid[0], preferred_element_type=F32)).astype(BF16)
    three = jnp.dot(two, w_out[0], preferred_element_type=F32).astype(BF16)
    back_slots[...] = three.reshape(2 * LON, 16, LEV)

    def send_back(t, carry):
        other = lax.rem(q + t, LON)
        pltpu.make_async_remote_copy(
            back_slots.at[pl.ds(other * 2, 2)],
            ret_slots.at[pl.ds(q * 2, 2)],
            send_sem.at[7],
            recv_sem.at[7],
            device_id=(p, other),
            device_id_type=MESH,
        ).start()
        return carry

    lax.fori_loop(1, LON, send_back, 0)
    pltpu.make_async_copy(
        back_slots.at[pl.ds(q * 2, 2)], ret_slots.at[pl.ds(q * 2, 2)], recv_sem.at[7]
    ).start()
    ret_slots[2 * LON] = jnp.zeros((16, LEV), BF16)
    some = pl.ds(0, 2 * LON)
    pltpu.make_async_copy(ret_slots.at[some], ret_slots.at[some], recv_sem.at[7]).wait()

    def unpack(r, carry):
        for k in range(5):
            heat[r, pl.ds(k * 16, 16), :] = ret_slots[place[r * 5 + k]]
        return carry

    lax.fori_loop(0, ROWS, unpack, 0)
    put_heat = pltpu.make_async_copy(heat, heating_hbm, local_sem.at[7])
    put_heat.start()

    sent = pl.ds(0, LAT - 1)
    pltpu.make_async_copy(pay.at[sent], pay.at[sent], send_sem.at[0]).wait()
    sent = pl.ds(0, LON - 1)
    pltpu.make_async_copy(slab.at[sent], slab.at[sent], send_sem.at[5]).wait()

    @pl.when(p < LAT - 1)
    def _():
        pltpu.make_async_copy(land_south, land_south, send_sem.at[8]).wait()

    @pl.when(p > 0)
    def _():
        pltpu.make_async_copy(land_north, land_north, send_sem.at[9]).wait()

    sent = pl.ds(0, 2 * LON - 2)
    pltpu.make_async_copy(out_slots.at[sent], out_slots.at[sent], send_sem.at[6]).wait()
    pltpu.make_async_copy(back_slots.at[sent], back_slots.at[sent], send_sem.at[7]).wait()
    put_adv.wait()
    put_heat.wait()


def hand_out(advected_hbm, heating_hbm, advected_out, heating_out, adv, heat, in_sem, out_sem):
    ways = []
    for k in range(2):
        part = pl.ds(k * (ROWS // 2), ROWS // 2)
        for source, held, target, at in (
            (advected_hbm, adv, advected_out, k),
            (heating_hbm, heat, heating_out, 2 + k),
        ):
            ways.append(
                (
                    pltpu.make_async_copy(source.at[part], held.at[part], in_sem.at[at]),
                    pltpu.make_async_copy(held.at[part], target.at[part], out_sem.at[at]),
                )
            )
    for there, _ in ways:
        there.start()
    for there, back in ways:
        there.wait()
        back.start()
    for _, back in ways:
        back.wait()


def body(
    spectral,
    wavenumber_of_slot,
    filter_strength,
    courant,
    sunlit_blocks,
    sunlit_owner,
    radiation_in,
    radiation_mid,
    radiation_out,
):
    smem = pl.BlockSpec(memory_space=pltpu.SMEM)
    anywhere = pl.BlockSpec(memory_space=pl.ANY)
    dma = pltpu.SemaphoreType.DMA
    outs = (
        jax.ShapeDtypeStruct((ROWS, COLS, LEV), F32),
        jax.ShapeDtypeStruct((ROWS, COLS, LEV), BF16),
    )
    advected, heating = pl.pallas_call(
        kernel,
        out_shape=outs,
        in_specs=[smem] * 4 + [anywhere] * 6,
        out_specs=(anywhere, anywhere),
        scratch_shapes=[
            pltpu.VMEM((ROWS, 2, OWN, DEG), BF16),
            pltpu.VMEM((LAT * 16, DEG), BF16),
            pltpu.VMEM((2, ROWS, COLS, LEV), BF16),
            pltpu.VMEM((1, LEV, HID), BF16),
            pltpu.VMEM((1, HID, HID), BF16),
            pltpu.VMEM((1, HID, LEV), BF16),
            pltpu.VMEM((256, DEG), BF16),
            pltpu.VMEM((LAT, PACK // 2, 2, LEV), BF16),
            pltpu.VMEM((LAT, PACK // 2, 2, LEV), BF16),
            pltpu.VMEM((LAT * PACK, LEV), F32),
            pltpu.VMEM((COLS, NLON), F32),
            pltpu.VMEM((COLS, NLON), BF16),
            pltpu.VMEM((LON // 4, NLON, 512), BF16),
            pltpu.VMEM((DEG, LEV), F32),
            pltpu.VMEM((LON, COLS, LEV), BF16),
            pltpu.VMEM((LON, COLS, LEV), BF16),
            pltpu.VMEM((LON, 16, LEV), BF16),
            pltpu.VMEM((LON, 16, LEV), BF16),
            pltpu.VMEM((2, COLS, LEV), BF16),
            pltpu.VMEM((2, COLS, LEV), BF16),
            pltpu.VMEM((2, ROWS, 16, LEV), BF16),
            pltpu.VMEM((2, ROWS, 16, LEV), BF16),
            pltpu.VMEM((2, ROWS + 2, WIDE, LEV), F32),
            pltpu.VMEM((ROWS + 4, WIDE, LEV), F32),
            pltpu.VMEM((ROWS + 2, WIDE, LEV), F32),
            pltpu.VMEM((ROWS, COLS, LEV), F32),
            pltpu.VMEM((50, 16, LEV), BF16),
            pltpu.VMEM((2 * LON, 16, LEV), BF16),
            pltpu.VMEM((2 * LON, 16, LEV), BF16),
            pltpu.VMEM((2 * LON, 16, LEV), BF16),
            pltpu.VMEM((2 * LON + 1, 16, LEV), BF16),
            pltpu.VMEM((ROWS, COLS, LEV), BF16),
            pltpu.SMEM((32,), jnp.int32),
            pltpu.SMEM((50,), jnp.int32),
            dma((8,)),
            dma((10,)),
            dma((10,)),
            pltpu.SemaphoreType.REGULAR,
        ],
        compiler_params=pltpu.CompilerParams(
            collective_id=1, has_side_effects=True, vmem_limit_bytes=64 * 1024 * 1024
        ),
        name="spectral_radiation",
    )(
        wavenumber_of_slot,
        filter_strength,
        sunlit_blocks.reshape(-1),
        sunlit_owner.reshape(-1),
        spectral,
        jnp.asarray(latitude_rows()),
        courant,
        radiation_in,
        radiation_mid,
        radiation_out,
    )
    return pl.pallas_call(
        hand_out,
        out_shape=outs,
        in_specs=[anywhere] * 2,
        out_specs=(anywhere, anywhere),
        scratch_shapes=[
            pltpu.VMEM((ROWS, COLS, LEV), F32),
            pltpu.VMEM((ROWS, COLS, LEV), BF16),
            dma((4,)),
            dma((4,)),
        ],
        name="hand_out",
        compiler_params=pltpu.CompilerParams(vmem_limit_bytes=64 * 1024 * 1024),
    )(advected, heating)


def solution(mesh):
    in_specs = (
        P("lat", None, "lon", None),
        P(),
        P("lon"),
        P(None, "lat", "lon", None),
        P("lat", "lon", None),
        P("lat", "lon", None, None),
        P("lon", None, None),
        P("lon", None, None),
        P("lon", None, None),
    )
    out_specs = (P("lat", "lon", None), P("lat", "lon", None))
    return jax.shard_map(body, mesh=mesh, in_specs=in_specs, out_specs=out_specs, check_vma=False)
```
